128 devices in a mesh: section: 8 (over y_lo, x), expert: 16 (over y_hi, z, core).
Axes of the slice: x: 4, y: 4 (y_hi: 2, y_lo: 2; y = y_hi * 2 + y_lo), z: 4, core: 2. Of those that a mesh axis runs over, the one named last changes fastest.
Arguments:
- fwd_acts: bfloat16 [8, 2048, 3584], P('section', 'expert'), may hold values from -6 to 6
- bwd_saved: bfloat16 [8, 2048, 3584], P('section', 'expert'), may hold values from -6 to 6
- bwd_cot: bfloat16 [8, 2048, 3584], P('section', 'expert'), may hold values from -6 to 6
- fwd_ids: int32 [8, 2048, 2], P('section', 'expert'), may hold values from 0 to 15, all different within a row; in each aligned block of 128 rows (0 to 127, 128 to 255, ..., all dimensions but the last counted through in order) at most 20 rows name the same one
- bwd_ids: int32 [8, 2048, 2], P('section', 'expert'), may hold values from 0 to 15, all different within a row; in each aligned block of 128 rows (0 to 127, 128 to 255, ..., all dimensions but the last counted through in order) at most 20 rows name the same one
- norm_gain: bfloat16 [8, 3584], P('section'), may hold values from 0.099609375 to 1.8984375
- router: bfloat16 [8, 3584, 16], P('section'), may hold values from -0.09375 to 0.09375
- w_gate: bfloat16 [8, 16, 3584, 1024], P('section', 'expert'), may hold values from -0.09375 to 0.09375
- w_up: bfloat16 [8, 16, 3584, 1024], P('section', 'expert'), may hold values from -0.09375 to 0.09375
- w_down: bfloat16 [8, 16, 1024, 3584], P('section', 'expert'), may hold values from -0.1875 to 0.1875
Outputs:
- fwd_out: bfloat16 [8, 2048, 3584], P('section', 'expert')
- bwd_grad: bfloat16 [8, 2048, 3584], P('section', 'expert')
The draws below stay inside these ranges and needn't reach their ends.
Inputs may be any that keep to these rules, and one draw needn't show every extreme that they name: `fwd_ids`: each token names 2 different experts; in each aligned block of 128 rows (the rows of one device) no expert is named by more than 20 rows, a bound that some block reaches. `bwd_ids`: each token names 2 different experts; in each aligned block of 128 rows (the rows of one device) no expert is named by more than 20 rows, a bound that some block reaches.
All inputs are finite; a program needn't handle non-finite values.
Results may differ from the reference program's by a relative error of at most 0.0066.
Values may be sent and summed in bfloat16 or wider, within the bound.
A program may use at most 128 MiB of HBM per device.

```python
import math
import jax
import jax.numpy as jnp
import numpy as np
from jax import lax

D = 3584
H = 1024
TOP = 2
TOK_DEV = 128
LAYERS = 8
EXPERTS = 16
TOKENS = 2048
CAP = 20


def level_of(rng, extent, split, low, top_value):
    level, own = 1.0, jax.random.fold_in(rng, 6)
    for axis_at, parts in split:
        heights = jnp.exp(jax.random.uniform(jax.random.fold_in(own, axis_at), (parts,), jnp.float32, low / len(split), top_value / len(split)))
        level = level * jnp.repeat(heights, extent[axis_at] // parts).reshape([-1 if axis == axis_at else 1 for axis in range(len(extent))])
    return level


def routed_block(rng, own, number, rows, count, top, most, lean):
    ranking = jax.random.permutation(rng, count)
    heavy_load, common = shares(count, rows * top, most, lean, True), shares(count, rows * top, most, lean, False)
    places = jnp.arange(count)

    def named(sizes, rotation):
        used = int((sizes > 0).sum())
        fixed = max(1, used // 4)
        moved = fixed + (places - fixed + rotation * (used - fixed)) % max(1, count - fixed)
        return jnp.zeros((count,), jnp.int32).at[ranking[jnp.where(places < fixed, places, moved)]].set(jnp.asarray(sizes, jnp.int32))

    sizes = jnp.where(number % 4 == 0, named(heavy_load, number // 4), named(common, number - number // 4 - 1))
    mixed = jax.random.permutation(jax.random.fold_in(own, 3), count)
    giver, taker = mixed[0:count // 2 * 2:2], mixed[1:count // 2 * 2:2]
    slack = jnp.minimum(sizes[giver] - 1, most - sizes[taker]) // 2
    slack = jnp.where((giver == ranking[0]) | (taker == ranking[0]) | (sizes[taker] == 0), 0, jnp.maximum(slack, 0))
    moved = jax.random.randint(jax.random.fold_in(own, 4), (count // 2,), 0, 1 << 20) % (slack + 1)
    sizes = sizes.at[giver].add(-moved).at[taker].add(moved)
    labels = jnp.searchsorted(jnp.cumsum(sizes), jnp.arange(rows * top), side="right").astype(jnp.int32)
    table = labels.reshape(top, rows).T
    table = table[jax.random.permutation(jax.random.fold_in(own, 1), rows)]
    rotation = jax.random.randint(jax.random.fold_in(own, 2), (rows, 1), 0, top)
    return jnp.take_along_axis(table, (jnp.arange(top)[None, :] + rotation) % top, axis=1)


def shares(number_of, total, limit, lean, full):
    weights = [(1 << 20) // math.isqrt(standing ** lean) + 1 for standing in range(1, number_of + 1)]
    largest = limit if full else min(limit, max(-(-total // number_of), total * weights[0] // sum(weights)))
    least = 1 if total - largest >= number_of - 1 else 0
    holding, spare = [largest] + [least] * (number_of - 1), total - largest - least * (number_of - 1)
    while spare > 0:
        free = [i for i in range(1, number_of) if holding[i] < largest] or [i for i in range(1, number_of) if holding[i] < limit]
        pool, left = sum([weights[i] for i in free]), spare
        for i in free:
            extra = min(limit - holding[i], max(1, left * weights[i] // pool), spare)
            holding[i] = holding[i] + extra
            spare = spare - extra
    return np.array(holding)


def gaussian(own_key, extent, deviation, reach, shards=(), held_as=jnp.bfloat16):
    factor_of = level_of(own_key, extent, shards, -0.22, 0.18) if shards else 1.0
    drawn = jax.random.normal(own_key, extent, jnp.float32) * deviation * factor_of
    return jnp.minimum(jnp.maximum(drawn, -reach), reach).astype(held_as)


def setup_inputs(seed: int = 0) -> dict:
    splits = jax.random.split(jax.random.key(seed), 11)
    fwd_acts = gaussian(splits[0], (LAYERS, TOKENS, D), 1.0, 6.0, ((0, 8), (1, 16)))
    bwd_saved = gaussian(splits[1], (LAYERS, TOKENS, D), 1.0, 6.0, ((0, 8), (1, 16)))
    bwd_cot = gaussian(splits[2], (LAYERS, TOKENS, D), 1.0, 6.0, ((0, 8), (1, 16)))
    fwd_ids_keys = jax.random.split(jax.random.fold_in(splits[3], 1), LAYERS * TOKENS // TOK_DEV)
    fwd_ids_turns = jax.random.permutation(jax.random.fold_in(splits[3], 3), LAYERS * TOKENS // TOK_DEV)
    fwd_ids = jax.vmap(lambda own, number: routed_block(jax.random.fold_in(splits[3], 2), own, number, TOK_DEV, EXPERTS, TOP, CAP, 1))(fwd_ids_keys, fwd_ids_turns).reshape((LAYERS, TOKENS, TOP))
    bwd_ids_keys = jax.random.split(jax.random.fold_in(splits[4], 1), LAYERS * TOKENS // TOK_DEV)
    bwd_ids_turns = jax.random.permutation(jax.random.fold_in(splits[4], 3), LAYERS * TOKENS // TOK_DEV)
    bwd_ids = jax.vmap(lambda own, number: routed_block(jax.random.fold_in(splits[4], 2), own, number, TOK_DEV, EXPERTS, TOP, CAP, 1))(bwd_ids_keys, bwd_ids_turns).reshape((LAYERS, TOKENS, TOP))
    norm_gain = jnp.clip(1.0 + 0.18 * jax.random.normal(splits[5], (LAYERS, D), jnp.float32), 0.099609375, 1.8984375).astype(jnp.bfloat16)
    router = gaussian(splits[6], (LAYERS, D, EXPERTS), D ** -0.5, 0.09375, ((0, 8),))
    w_gate = gaussian(splits[7], (LAYERS, EXPERTS, D, H), D ** -0.5, 0.09375, ((0, 8), (1, 16)))
    w_up = gaussian(splits[8], (LAYERS, EXPERTS, D, H), D ** -0.5, 0.09375, ((0, 8), (1, 16)))
    w_down = gaussian(splits[9], (LAYERS, EXPERTS, H, D), H ** -0.5, 0.1875, ((0, 8), (1, 16)))
    return dict(fwd_acts=fwd_acts, bwd_saved=bwd_saved, bwd_cot=bwd_cot, fwd_ids=fwd_ids, bwd_ids=bwd_ids, norm_gain=norm_gain, router=router, w_gate=w_gate, w_up=w_up, w_down=w_down)


route_scale = 2.5
epsilon = 1e-06

def normalize(x, gain):
    xf = x.astype(jnp.float32)
    inv = lax.rsqrt(lax.optimization_barrier(jnp.mean(xf * xf, axis=-1, keepdims=True)) + epsilon)
    normed = (xf * inv * gain.astype(jnp.float32)).astype(jnp.bfloat16)
    return (xf, inv, normed)

def gating(normed, route_w, ids):
    logits = jnp.dot(normed, route_w, preferred_element_type=jnp.float32)
    count = route_w.shape[-1]
    hot = (ids[:, :, None] == jnp.arange(count, dtype=jnp.int32)[None, None, :]).astype(jnp.float32)
    chosen = lax.optimization_barrier(jnp.sum(hot * logits[:, None, :], axis=-1))
    score = jax.nn.sigmoid(chosen)
    total = lax.optimization_barrier(jnp.sum(score, axis=-1, keepdims=True))
    weight = route_scale * score / total
    return (hot, score, total, weight)

def expert_forward(rows, wg, wu, wd):
    gate = jnp.dot(rows, wg, preferred_element_type=jnp.float32)
    upper = jnp.dot(rows, wu, preferred_element_type=jnp.float32)
    act = (gate * jax.nn.sigmoid(gate) * upper).astype(jnp.bfloat16)
    return lax.optimization_barrier(jnp.dot(act, wd, preferred_element_type=jnp.float32).astype(jnp.bfloat16))

def expert_backward(rows, cot, wg, wu, wd):
    gate = jnp.dot(rows, wg, preferred_element_type=jnp.float32)
    upper = jnp.dot(rows, wu, preferred_element_type=jnp.float32)
    sig = jax.nn.sigmoid(gate)
    act = (gate * sig * upper).astype(jnp.bfloat16)
    output = lax.optimization_barrier(jnp.dot(act, wd, preferred_element_type=jnp.float32).astype(jnp.bfloat16))
    grad_act = jnp.dot(cot, wd.T, preferred_element_type=jnp.float32)
    dgate = (grad_act * upper * sig * (1.0 + gate * (1.0 - sig))).astype(jnp.bfloat16)
    dup = (grad_act * gate * sig).astype(jnp.bfloat16)
    unit = jnp.dot(dgate, wg.T, preferred_element_type=jnp.float32) + jnp.dot(dup, wu.T, preferred_element_type=jnp.float32)
    unit = unit.astype(jnp.bfloat16)
    product = lax.optimization_barrier(jnp.sum(output.astype(jnp.float32) * cot.astype(jnp.float32), axis=-1)).astype(jnp.bfloat16)
    return lax.optimization_barrier((unit, product))

def select_rows(flat_ids, index):
    marked = flat_ids == index
    order = jnp.argsort(jnp.where(marked, 0, 1).astype(jnp.int32), stable=True)[:EXPERTS * CAP].astype(jnp.int32)
    valid = marked[order]
    token = (order // TOP).astype(jnp.int32)
    return (order, valid, token)

def section_work(items):
    h_in, saved, cot, ids_f, ids_b, gain, route_w, gates_w, ups_w, downs_w = items
    width = h_in.shape[-1]
    expert_range = jnp.arange(EXPERTS, dtype=jnp.int32)
    xf, inv_f, normed_f = normalize(h_in, gain)
    hot_f, score_f, total_f, weight_f = gating(normed_f, route_w, ids_f)
    flat_f = ids_f.reshape(-1)

    def forward_expert(acc, pieces):
        index, wg, wu, wd = pieces
        order, valid, token = select_rows(flat_f, index)
        output = expert_forward(normed_f[token], wg, wu, wd)
        acc = acc.at[order].add(jnp.where(valid[:, None], output.astype(jnp.float32), 0.0))
        return (acc, None)
    start_f = jnp.zeros((flat_f.shape[0], width), jnp.float32)
    acc_f, _ = lax.scan(forward_expert, start_f, (expert_range, gates_w, ups_w, downs_w))
    mixed = lax.optimization_barrier(jnp.sum(weight_f[..., None] * acc_f.reshape(ids_f.shape + (width,)), axis=1))
    fwd_out = (xf + mixed).astype(jnp.bfloat16)
    xb, inv_b, normed_b = normalize(saved, gain)
    hot_b, score_b, total_b, weight_b = gating(normed_b, route_w, ids_b)
    flat_b = ids_b.reshape(-1)

    def backward_expert(acc, pieces):
        index, wg, wu, wd = pieces
        acc_unit, acc_prod = acc
        order, valid, token = select_rows(flat_b, index)
        unit, product = expert_backward(normed_b[token], cot[token], wg, wu, wd)
        acc_unit = acc_unit.at[order].add(jnp.where(valid[:, None], unit.astype(jnp.float32), 0.0))
        acc_prod = acc_prod.at[order].add(jnp.where(valid, product.astype(jnp.float32), 0.0))
        return ((acc_unit, acc_prod), None)
    start_b = (jnp.zeros((flat_b.shape[0], width), jnp.float32), jnp.zeros((flat_b.shape[0],), jnp.float32))
    (acc_unit, acc_prod), _ = lax.scan(backward_expert, start_b, (expert_range, gates_w, ups_w, downs_w))
    unit_all = acc_unit.reshape(ids_b.shape + (width,))
    product = acc_prod.reshape(ids_b.shape)
    from_experts = lax.optimization_barrier(jnp.sum(weight_b[..., None] * unit_all, axis=1))
    dscore = route_scale / total_b * (product - lax.optimization_barrier(jnp.sum(product * weight_b, axis=-1, keepdims=True)) / route_scale)
    dlogit = dscore * score_b * (1.0 - score_b)
    dlogits = lax.optimization_barrier(jnp.sum(hot_b * dlogit[..., None], axis=1)).astype(jnp.bfloat16)
    dnormed = from_experts + jnp.dot(dlogits, route_w.T, preferred_element_type=jnp.float32)
    scaled = gain.astype(jnp.float32) * dnormed
    dx = inv_b * scaled - xb * inv_b ** 3 * lax.optimization_barrier(jnp.mean(xb * scaled, axis=-1, keepdims=True))
    bwd_grad = (cot.astype(jnp.float32) + dx).astype(jnp.bfloat16)
    return (fwd_out, bwd_grad)

def reference(fwd_acts, bwd_saved, bwd_cot, fwd_ids, bwd_ids, norm_gain, router, w_gate, w_up, w_down):
    arrive_f = jnp.roll(fwd_acts, 1, axis=0)
    arrive_b = jnp.roll(bwd_cot, -1, axis=0)
    fwd_out, bwd_grad = lax.map(section_work, (arrive_f, bwd_saved, arrive_b, fwd_ids, bwd_ids, norm_gain, router, w_gate, w_up, w_down))
    return (fwd_out, bwd_grad)
```

```python
import functools

import jax
import jax.numpy as jnp
from jax import lax
from jax.experimental import pallas as pl
from jax.experimental.pallas import tpu as pltpu
from jax.sharding import PartitionSpec as P

MESH = pl.DeviceIdType.MESH
F32, BF16 = jnp.float32, jnp.bfloat16
route_scale = 2.5
epsilon = 1e-06

D, H, T, E = 3584, 1024, 128, 16
MAIN, OVER, PARTS = 16, 4, 4
WIDE = D // PARTS
BLOCK = MAIN * PARTS + OVER * PARTS
ROWS = E * (MAIN + OVER)
HALF = E // 2
HTILE = 256
NONE = -1000.0


def nt(a, b):
    return lax.dot_general(a, b, (((1,), (1,)), ((), ())), preferred_element_type=F32)


def nn(a, b):
    return jnp.dot(a, b, preferred_element_type=F32)


def iota(shape, axis):
    return lax.broadcasted_iota(jnp.int32, shape, axis)


def route(ids):
    lanes = iota((T, T), 1)
    hot = [(lanes == ids[:, k : k + 1]).astype(F32) for k in (0, 1)]
    tri = (iota((T, T), 0) > lanes).astype(BF16)
    before = nn(tri, (hot[0] + hot[1]).astype(BF16))
    packed = jnp.full((T, T), NONE, F32)
    for k in (0, 1):
        slot = jnp.sum(hot[k] * before, axis=1, keepdims=True)
        base = (ids[:, k : k + 1] * MAIN).astype(F32)
        packed = jnp.where(lanes == k, jnp.where(slot < MAIN, base + slot, NONE), packed)
        packed = jnp.where(lanes == 2 + k, jnp.where(slot < MAIN, NONE, base + slot - MAIN), packed)
    return packed


def picks(rows, places, base, shift):
    at = (iota((T, T), 0) + base).astype(F32)
    return sum((at == rows[p : p + 1, :] + shift).astype(F32) for p in places).astype(BF16)


def gates(logits, ids):
    lanes = iota((T, E), 1)
    score = [
        jax.nn.sigmoid(jnp.sum(jnp.where(lanes == ids[:, k : k + 1], logits, 0.0), axis=1, keepdims=True))
        for k in (0, 1)
    ]
    total = score[0] + score[1]
    return score, total, [route_scale * s / total for s in score]


def spread(places, values, shift):
    at = iota((T, E * MAIN), 1).astype(F32)
    return sum(jnp.where(at == p + shift, v, 0.0) for p, v in zip(places, values)).astype(BF16)


def kernel(
    fwd_hbm, saved_hbm, cot_hbm, idf_hbm, idb_hbm, gain_hbm, router_hbm, wg_hbm, wu_hbm, wd_hbm,
    of_hbm, ob_hbm,
    wg, wu, wd, a1s, a1r, a2s, a2r, a3s, a3r, r1r, r2r, ps, pr,
    xr, cr, saved, normed, arr_f, arr_b, dg, du, scaled, router, gain, idf, idb, colf, colb, gf, gb,
    ssem, rsem, hsem, lsem, osem,
):
    s, e = lax.axis_index("section"), lax.axis_index("expert")
    layers = lax.axis_size("section")
    after, ahead = (s + 1) % layers, (s + layers - 1) % layers
    yhi = e // HALF

    loads = [
        pltpu.make_async_copy(src, dst, lsem.at[i])
        for i, (src, dst) in enumerate(
            [(saved_hbm, saved), (idb_hbm, idb), (gain_hbm, gain), (idf_hbm, idf), (router_hbm, router),
             (wg_hbm, wg), (wu_hbm, wu), (wd_hbm, wd)]
        )
    ]
    for load in loads[:3]:
        load.start()

    barrier = pltpu.get_barrier_semaphore()

    def greet(d, _):
        pl.semaphore_signal(barrier, inc=1, device_id=(s, (e + d) % E), device_id_type=MESH)
        return 0

    lax.fori_loop(1, E, greet, 0)
    for t in (after, ahead):
        pl.semaphore_signal(barrier, inc=1, device_id=(t, e), device_id_type=MESH)
    pl.semaphore_wait(barrier, E + 1)

    hop_f = pltpu.make_async_remote_copy(
        fwd_hbm, arr_f, hsem.at[0], hsem.at[1], device_id=(after, e), device_id_type=MESH)
    hop_b = pltpu.make_async_remote_copy(
        cot_hbm, arr_b, hsem.at[2], hsem.at[3], device_id=(ahead, e), device_id_type=MESH)
    hop_b.start()
    hop_f.start()
    for load in loads[3:]:
        load.start()

    def remote(k, src, dst, p, at):
        return pltpu.make_async_remote_copy(
            src.at[p], dst.at[at], ssem.at[k, p], rsem.at[k, at], device_id=(s, p), device_id_type=MESH)

    def own(k, src, dst):
        return pltpu.make_async_copy(src.at[e], dst.at[e], rsem.at[k, e])

    def send(k, src, dst, first, last):
        def step(d, _):
            remote(k, src, dst, (e + d) % E, e).start()
            return 0

        if first == 0:
            own(k, src, dst).start()
        lax.fori_loop(max(first, 1), last, step, 0)

    def send_half(k, src, dst, half):
        def step(i, _):
            p = half * HALF + (e + i) % HALF
            remote(k, src, dst, p, e).start()
            return 0

        lax.fori_loop(1, HALF, step, 0)

    def arrive(k, src, dst):
        def step(d, _):
            p = (e + d) % E
            remote(k, src, dst, p, p).wait_recv()
            return 0

        lax.fori_loop(1, E, step, 0)
        own(k, src, dst).wait()

    def sent(k, src, dst):
        def step(d, _):
            remote(k, src, dst, (e + d) % E, e).wait_send()
            return 0

        lax.fori_loop(1, E, step, 0)

    def norm(x_ref, out):
        x = x_ref[...].astype(F32)
        inv = lax.rsqrt(jnp.sum(x * x, axis=1, keepdims=True) * (1.0 / D) + epsilon)
        out[...] = (x * inv * gain[...].astype(F32)).astype(BF16)
        return inv

    def pack(x_ref, rows, buf, half):
        base = half * (HALF * MAIN)
        main = picks(rows, (0, 1), base, 0.0)

        def step(q, _):
            got = nn(main, x_ref[:, pl.ds(pl.multiple_of(q * WIDE, 128), WIDE)]).astype(BF16)
            buf[pl.ds(half * HALF, HALF), pl.ds(pl.multiple_of(q * MAIN, MAIN), MAIN), :] = got.reshape(HALF, MAIN, WIDE)
            return 0

        lax.fori_loop(0, PARTS, step, 0)
        over = sum(
            nn(picks(rows, (2, 3), base, float(OVER * q)), x_ref[:, q * WIDE : (q + 1) * WIDE])
            for q in range(PARTS)
        )
        buf[pl.ds(half * HALF, HALF), MAIN * PARTS : BLOCK, :] = over.astype(BF16).reshape(HALF, MAIN, WIDE)

    def dispatch(k, x_ref, rows, src, dst):
        for near in (True, False):
            half = yhi if near else 1 - yhi
            pack(x_ref, rows, src, half)
            if near:
                own(k, src, dst).start()
                send_half(k, src, dst, half)
            else:
                send_half(k, src, dst, half)
                remote(k, src, dst, half * HALF + e % HALF, e).start()

    def unpack(buf, out):
        tail = buf[:, MAIN * PARTS : BLOCK, :].reshape(E * MAIN, WIDE)
        row, lane = iota((E * OVER, E * MAIN), 0), iota((E * OVER, E * MAIN), 1)

        def step(q, _):
            columns = pl.ds(pl.multiple_of(q * WIDE, 128), WIDE)
            out[0 : E * MAIN, columns] = buf[:, pl.ds(pl.multiple_of(q * MAIN, MAIN), MAIN), :].reshape(E * MAIN, WIDE)
            pick = (lane == (row // OVER) * MAIN + OVER * q + row % OVER).astype(BF16)
            out[E * MAIN : ROWS, columns] = nn(pick, tail).astype(BF16)
            return 0

        lax.fori_loop(0, PARTS, step, 0)

    def lay(q, buf, value):
        low = value.astype(BF16)
        buf[:, pl.ds(pl.multiple_of(q * MAIN, MAIN), MAIN), :] = low[0 : E * MAIN].reshape(E, MAIN, WIDE)
        row, lane = iota((E * MAIN, E * OVER), 0), iota((E * MAIN, E * OVER), 1)
        here = (lane == (row // MAIN) * OVER + row % OVER) & (row % MAIN // OVER == q)
        return nn(here.astype(BF16), low[E * MAIN : ROWS])

    for load in loads[:3]:
        load.wait()
    inv_b = norm(saved, normed)
    gb[:, 0:1] = inv_b
    packed = route(idb[...])
    colb[...] = packed
    rows_b = jnp.transpose(packed)[0:8, :]
    dispatch(0, normed, rows_b, a1s, a1r)
    loads[4].wait()
    score, total, weight = gates(nn(normed[...], router[...]), idb[...])
    gb[:, 1:2], gb[:, 2:3], gb[:, 3:4] = score[0], score[1], total
    gb[:, 4:5], gb[:, 5:6] = weight[0], weight[1]

    hop_b.wait_recv()
    dispatch(1, arr_b, rows_b, a2s, a2r)

    loads[3].wait()
    hop_f.wait_recv()
    norm(arr_f, normed)
    packed = route(idf[...])
    colf[...] = packed
    dispatch(2, normed, jnp.transpose(packed)[0:8, :], a3s, a3r)
    score, total, weight = gates(nn(normed[...], router[...]), idf[...])
    gf[:, 0:1], gf[:, 1:2] = weight[0], weight[1]

    for load in loads[5:]:
        load.wait()
    arrive(0, a1s, a1r)
    unpack(a1r, xr)
    arrive(1, a2s, a2r)
    unpack(a2r, cr)

    def hidden(n, prod):
        columns = pl.ds(pl.multiple_of(n * HTILE, HTILE), HTILE)
        gate, up = nn(xr[...], wg[:, columns]), nn(xr[...], wu[:, columns])
        grad = nt(cr[...], wd[columns, :])
        sig = jax.nn.sigmoid(gate)
        act = (gate * sig * up).astype(BF16).astype(F32)
        dg[:, columns] = (grad * up * sig * (1.0 + gate * (1.0 - sig))).astype(BF16)
        du[:, columns] = (grad * gate * sig).astype(BF16)
        return prod + jnp.sum(act * grad, axis=1, keepdims=True)

    prod = lax.fori_loop(0, H // HTILE, hidden, jnp.zeros((ROWS, 1), F32))
    prod = jnp.broadcast_to(prod, (ROWS, T)).astype(BF16)
    ps[:, 0:MAIN, :] = prod[0 : E * MAIN].reshape(E, MAIN, T)
    row, lane = iota((E * MAIN, E * OVER), 0), iota((E * MAIN, E * OVER), 1)
    here = (lane == (row // MAIN) * OVER + row % OVER).astype(BF16)
    ps[:, MAIN : 2 * MAIN, :] = nn(here, prod[E * MAIN : ROWS]).astype(BF16).reshape(E, MAIN, T)
    send(3, ps, pr, 0, E)

    sent(0, a1s, a1r)

    def unit(q, over):
        rows = pl.ds(pl.multiple_of(q * WIDE, 128), WIDE)
        return over + lay(q, a1s, nt(dg[...], wg[rows, :]) + nt(du[...], wu[rows, :]))

    over = lax.fori_loop(0, PARTS, unit, jnp.zeros((E * MAIN, WIDE), F32))
    a1s[:, MAIN * PARTS : BLOCK, :] = over.astype(BF16).reshape(E, MAIN, WIDE)
    send(4, a1s, r1r, 0, E)

    arrive(2, a3s, a3r)
    unpack(a3r, xr)

    def hidden_f(n, _):
        columns = pl.ds(pl.multiple_of(n * HTILE, HTILE), HTILE)
        gate, up = nn(xr[...], wg[:, columns]), nn(xr[...], wu[:, columns])
        dg[:, columns] = (gate * jax.nn.sigmoid(gate) * up).astype(BF16)
        return 0

    lax.fori_loop(0, H // HTILE, hidden_f, 0)
    sent(1, a2s, a2r)

    def down(q, over):
        columns = pl.ds(pl.multiple_of(q * WIDE, 128), WIDE)
        return over + lay(q, a2s, nn(dg[...], wd[:, columns]))

    over = lax.fori_loop(0, PARTS, down, jnp.zeros((E * MAIN, WIDE), F32))
    a2s[:, MAIN * PARTS : BLOCK, :] = over.astype(BF16).reshape(E, MAIN, WIDE)
    send(5, a2s, r2r, 0, E)

    arrive(3, ps, pr)
    arrive(4, a1s, r1r)
    places = [colb[:, p : p + 1] for p in range(4)]
    score, total = [gb[:, 1:2], gb[:, 2:3]], gb[:, 3:4]
    weight = [gb[:, 4:5], gb[:, 5:6]]
    inv = gb[:, 0:1]
    one = jnp.ones((T, 1), F32)
    product = []
    for k in (0, 1):
        got = nn(spread([places[k]], [one], 0.0), pr[:, 0:MAIN, :].reshape(E * MAIN, T))
        got += nn(spread([places[2 + k]], [one], 0.0), pr[:, MAIN : 2 * MAIN, :].reshape(E * MAIN, T))
        product.append(got[:, 0:1])
    mixed = (product[0] * weight[0] + product[1] * weight[1]) * (1.0 / route_scale)
    lanes = iota((T, E), 1)
    dlogits = jnp.zeros((T, E), F32)
    for k in (0, 1):
        dlogit = route_scale / total * (product[k] - mixed) * score[k] * (1.0 - score[k])
        dlogits += jnp.where(lanes == idb[:, k : k + 1], dlogit, 0.0)
    dlogits = dlogits.astype(BF16)
    main_w = spread(places[0:2], weight, 0.0)

    def grad_in(q, dot):
        columns = pl.ds(pl.multiple_of(q * WIDE, 128), WIDE)
        over_w = spread(places[2:4], weight, (OVER * q).astype(F32))
        got = nn(main_w, r1r[:, pl.ds(pl.multiple_of(q * MAIN, MAIN), MAIN), :].reshape(E * MAIN, WIDE))
        got += nn(over_w, r1r[:, MAIN * PARTS : BLOCK, :].reshape(E * MAIN, WIDE))
        got += nt(dlogits, router[pl.ds(pl.multiple_of(q * WIDE, 128), WIDE), :])
        got *= gain[:, columns].astype(F32)
        scaled[:, columns] = got
        return dot + jnp.sum(got * saved[:, columns].astype(F32), axis=1, keepdims=True)

    dot = lax.fori_loop(0, PARTS, grad_in, jnp.zeros((T, 1), F32)) * (1.0 / D)
    back = inv * inv * inv * dot

    def finish_b(q, _):
        columns = pl.ds(pl.multiple_of(q * WIDE, 128), WIDE)
        dx = inv * scaled[:, columns] - saved[:, columns].astype(F32) * back
        saved[:, columns] = (arr_b[:, columns].astype(F32) + dx).astype(BF16)
        return 0

    lax.fori_loop(0, PARTS, finish_b, 0)
    out_b = pltpu.make_async_copy(saved, ob_hbm, osem.at[0])
    out_b.start()

    places_f = [colf[:, p : p + 1] for p in range(4)]
    weight_f = [gf[:, 0:1], gf[:, 1:2]]
    main_f = spread(places_f[0:2], weight_f, 0.0)
    arrive(5, a2s, r2r)

    def finish_f(q, _):
        columns = pl.ds(pl.multiple_of(q * WIDE, 128), WIDE)
        over_w = spread(places_f[2:4], weight_f, (OVER * q).astype(F32))
        got = nn(main_f, r2r[:, pl.ds(pl.multiple_of(q * MAIN, MAIN), MAIN), :].reshape(E * MAIN, WIDE))
        got += nn(over_w, r2r[:, MAIN * PARTS : BLOCK, :].reshape(E * MAIN, WIDE))
        normed[:, columns] = (arr_f[:, columns].astype(F32) + got).astype(BF16)
        return 0

    lax.fori_loop(0, PARTS, finish_f, 0)
    out_f = pltpu.make_async_copy(normed, of_hbm, osem.at[1])
    out_f.start()
    hop_f.wait_send()
    hop_b.wait_send()
    sent(2, a3s, a3r)
    sent(3, ps, pr)
    sent(4, a1s, r1r)
    sent(5, a2s, r2r)
    out_b.wait()
    out_f.wait()


def per_device(fwd_acts, bwd_saved, bwd_cot, fwd_ids, bwd_ids, norm_gain, router, w_gate, w_up, w_down):
    def vm(*shape, dtype=BF16):
        return pltpu.VMEM(shape, dtype)

    block = (E, BLOCK, WIDE)
    scratch = [
        vm(D, H), vm(D, H), vm(H, D),
        *[vm(*block) for _ in range(8)],
        vm(E, 2 * MAIN, T), vm(E, 2 * MAIN, T),
        vm(ROWS, D), vm(ROWS, D),
        vm(T, D), vm(T, D), vm(T, D), vm(T, D),
        vm(ROWS, H), vm(ROWS, H),
        vm(T, D, dtype=F32),
        vm(D, E), vm(1, D),
        vm(T, 2, dtype=jnp.int32), vm(T, 2, dtype=jnp.int32),
        vm(T, T, dtype=F32), vm(T, T, dtype=F32), vm(T, T, dtype=F32), vm(T, T, dtype=F32),
        pltpu.SemaphoreType.DMA((6, E)), pltpu.SemaphoreType.DMA((6, E)),
        pltpu.SemaphoreType.DMA((4,)), pltpu.SemaphoreType.DMA((8,)), pltpu.SemaphoreType.DMA((2,)),
    ]
    out = jax.ShapeDtypeStruct((T, D), BF16)
    fwd_out, bwd_grad = pl.pallas_call(
        kernel,
        out_shape=(out, out),
        in_specs=[pl.BlockSpec(memory_space=pl.ANY)] * 10,
        out_specs=(pl.BlockSpec(memory_space=pl.ANY),) * 2,
        scratch_shapes=scratch,
        name="layer",
        compiler_params=pltpu.CompilerParams(
            collective_id=0, has_side_effects=True, vmem_limit_bytes=62 * 1024 * 1024
        ),
        cost_estimate=pl.CostEstimate(flops=8 * 2 * ROWS * D * H, bytes_accessed=30_000_000, transcendentals=0),
    )(
        fwd_acts[0], bwd_saved[0], bwd_cot[0], fwd_ids[0], bwd_ids[0], norm_gain, router[0],
        w_gate[0, 0], w_up[0, 0], w_down[0, 0],
    )
    return fwd_out[None], bwd_grad[None]


def solution(mesh):
    rows = P("section", "expert", None)
    return jax.shard_map(
        per_device,
        mesh=mesh,
        in_specs=(
            rows, rows, rows, rows, rows, P("section", None), P("section", None, None),
            P("section", "expert", None, None), P("section", "expert", None, None), P("section", "expert", None, None),
        ),
        out_specs=(rows, rows),
        check_vma=False,
    )
```

```python
import functools

import jax
import jax.numpy as jnp
from jax import lax
from jax.experimental import pallas as pl
from jax.experimental.pallas import tpu as pltpu
from jax.sharding import PartitionSpec as P

MESH = pl.DeviceIdType.MESH
F32, BF16 = jnp.float32, jnp.bfloat16
route_scale = 2.5
epsilon = 1e-06

D, H, T, E = 3584, 1024, 128, 16
MAIN, OVER, PARTS = 16, 4, 4
WIDE = D // PARTS
BLOCK = MAIN * PARTS + OVER * PARTS
ROWS = E * (MAIN + OVER)
HALF = E // 2
HTILE = 256
NONE = -1000.0


def nt(a, b):
    return lax.dot_general(a, b, (((1,), (1,)), ((), ())), preferred_element_type=F32)


def nn(a, b):
    return jnp.dot(a, b, preferred_element_type=F32)


def iota(shape, axis):
    return lax.broadcasted_iota(jnp.int32, shape, axis)


def route(ids):
    at = iota((E, T), 0)
    hot = [(at == ids[k : k + 1, :]).astype(F32) for k in (0, 1)]
    tri = (iota((T, T), 0) < iota((T, T), 1)).astype(BF16)
    before = nn((hot[0] + hot[1]).astype(BF16), tri)
    line = iota((8, T), 0)
    rows = jnp.zeros((8, T), F32)
    for k in (0, 1):
        slot = jnp.sum(hot[k] * before, axis=0, keepdims=True)
        named = ids[k : k + 1, :].astype(F32)
        base = named * float(MAIN)
        rows = jnp.where(line == k, jnp.where(slot < MAIN, base + slot, NONE), rows)
        rows = jnp.where(line == 2 + k, jnp.where(slot < MAIN, NONE, base + slot - MAIN), rows)
        rows = jnp.where(line == 4 + k, named, rows)
    return rows


def stand(rows):
    return jnp.transpose(jnp.concatenate([rows, jnp.zeros((T - 8, T), F32)], axis=0))


def picks(rows, places, base, shift):
    at = (iota((T, T), 0) + base).astype(F32)
    return sum((at == rows[p : p + 1, :] + shift).astype(F32) for p in places).astype(BF16)


def gates(logits, columns):
    lanes = iota((T, E), 1).astype(F32)
    score = [
        jax.nn.sigmoid(jnp.sum(jnp.where(lanes == columns[:, 4 + k : 5 + k], logits, 0.0), axis=1, keepdims=True))
        for k in (0, 1)
    ]
    total = score[0] + score[1]
    return score, total, [route_scale * s / total for s in score]


def spread(places, values, shift):
    at = iota((T, E * MAIN), 1).astype(F32)
    return sum(jnp.where(at == p + shift, v, 0.0) for p, v in zip(places, values)).astype(BF16)


def kernel(
    fwd_hbm, saved_hbm, cot_hbm, idf_hbm, idb_hbm, gain_hbm, router_hbm, wg_hbm, wu_hbm, wd_hbm,
    of_hbm, ob_hbm,
    wg, wu, wd, a1s, a1r, a2s, a2r, a3s, a3r, r1r, r2r, ps, pr,
    xr, cr, saved, normed, arr_f, arr_b, dg, du, gates_b, ups_b, scaled, router, gain,
    idf, idb, rowf, rowb, colf, colb, gf, gb,
    ssem, rsem, hsem, lsem, osem,
):
    s, e = lax.axis_index("section"), lax.axis_index("expert")
    layers = lax.axis_size("section")
    after, ahead = (s + 1) % layers, (s + layers - 1) % layers
    yhi, zed, core = e // HALF, e // 2 % 4, e % 2
    near, far = yhi * HALF, (1 - yhi) * HALF

    loads = [
        pltpu.make_async_copy(src, dst, lsem.at[i])
        for i, (src, dst) in enumerate(
            [(saved_hbm, saved), (idb_hbm, idb), (gain_hbm, gain), (idf_hbm, idf),
             (router_hbm, router), (wg_hbm, wg), (wu_hbm, wu), (wd_hbm, wd)]
        )
    ]
    for load in loads[:4]:
        load.start()

    barrier = pltpu.get_barrier_semaphore()

    def greet(d, _):
        pl.semaphore_signal(barrier, inc=1, device_id=(s, (e + d) % E), device_id_type=MESH)
        return 0

    for t in (after, ahead):
        pl.semaphore_signal(barrier, inc=1, device_id=(t, e), device_id_type=MESH)
    lax.fori_loop(1, E, greet, 0)

    def hop(src, dst, i, t):
        return pltpu.make_async_remote_copy(
            src, dst, hsem.at[2 * i], hsem.at[2 * i + 1], device_id=(t, e), device_id_type=MESH)

    hop_f, hop_b = hop(fwd_hbm, arr_f, 0, after), hop(cot_hbm, arr_b, 1, ahead)

    def near_peer(i):
        return near + (zed + i // 2 + 1) % 4 * 2 + (core + i + 1) % 2

    def far_peer(i):
        return far + (zed + 2 + i // 2 * 3) % 4 * 2 + (core + i) % 2

    def near_from(i):
        return near + (zed + 3 - i // 2) % 4 * 2 + (core + i + 1) % 2

    def far_from(i):
        return far + (zed + 2 + i // 2) % 4 * 2 + (core + i) % 2

    def remote(k, src, dst, p, at):
        return pltpu.make_async_remote_copy(
            src.at[p], dst.at[at], ssem.at[k, p], rsem.at[k, at], device_id=(s, p), device_id_type=MESH)

    def own(k, src, dst):
        return pltpu.make_async_copy(src.at[e], dst.at[e], rsem.at[k, e])

    def each(count, act):
        def step(i, _):
            act(i)
            return 0

        lax.fori_loop(0, count, step, 0)

    def send_far(k, src, dst):
        each(HALF, lambda i: remote(k, src, dst, far_peer(i), e).start())

    def send_near(k, src, dst):
        each(HALF - 1, lambda i: remote(k, src, dst, near_peer(i), e).start())
        own(k, src, dst).start()

    def send(k, src, dst):
        send_far(k, src, dst)
        send_near(k, src, dst)

    def arrive(k, src, dst):
        def wait(p):
            remote(k, src, dst, p, p).wait_recv()

        each(HALF - 1, lambda i: wait(near_from(i)))
        each(HALF, lambda i: wait(far_from(i)))
        own(k, src, dst).wait()

    def sent(k, src, dst):
        def wait(p):
            remote(k, src, dst, p, e).wait_send()

        each(HALF - 1, lambda i: wait(near_peer(i)))
        each(HALF, lambda i: wait(far_peer(i)))

    def norm(x_ref, by, out):
        x = x_ref[...].astype(F32)
        inv = lax.rsqrt(jnp.sum(x * x, axis=1, keepdims=True) * (1.0 / D) + epsilon)
        out[...] = (x * inv * by[...].astype(F32)).astype(BF16)
        return inv

    def pack(x_ref, rows, buf, first):
        base = first * MAIN
        main = picks(rows, (0, 1), base, 0.0)

        def step(q, _):
            got = nn(main, x_ref[:, pl.ds(pl.multiple_of(q * WIDE, 128), WIDE)]).astype(BF16)
            buf[pl.ds(first, HALF), pl.ds(pl.multiple_of(q * MAIN, MAIN), MAIN), :] = got.reshape(HALF, MAIN, WIDE)
            return 0

        lax.fori_loop(0, PARTS, step, 0)
        over = sum(
            nn(picks(rows, (2, 3), base, float(OVER * q)), x_ref[:, q * WIDE : (q + 1) * WIDE])
            for q in range(PARTS)
        )
        buf[pl.ds(first, HALF), MAIN * PARTS : BLOCK, :] = over.astype(BF16).reshape(HALF, MAIN, WIDE)

    def dispatch(k, x_ref, rows, src, dst):
        pack(x_ref, rows, src, far)
        send_far(k, src, dst)
        pack(x_ref, rows, src, near)
        send_near(k, src, dst)

    def unpack(buf, out):
        tail = buf[:, MAIN * PARTS : BLOCK, :].reshape(E * MAIN, WIDE)
        row, lane = iota((E * OVER, E * MAIN), 0), iota((E * OVER, E * MAIN), 1)

        def step(q, _):
            columns = pl.ds(pl.multiple_of(q * WIDE, 128), WIDE)
            out[0 : E * MAIN, columns] = buf[:, pl.ds(pl.multiple_of(q * MAIN, MAIN), MAIN), :].reshape(E * MAIN, WIDE)
            pick = (lane == (row // OVER) * MAIN + OVER * q + row % OVER).astype(BF16)
            out[E * MAIN : ROWS, columns] = nn(pick, tail).astype(BF16)
            return 0

        lax.fori_loop(0, PARTS, step, 0)

    def lay(q, buf, value):
        low = value.astype(BF16)
        buf[:, pl.ds(pl.multiple_of(q * MAIN, MAIN), MAIN), :] = low[0 : E * MAIN].reshape(E, MAIN, WIDE)
        row, lane = iota((E * MAIN, E * OVER), 0), iota((E * MAIN, E * OVER), 1)
        here = (lane == (row // MAIN) * OVER + row % OVER) & (row % MAIN // OVER == q)
        return nn(here.astype(BF16), low[E * MAIN : ROWS])

    scope = jax.named_scope
    with scope("start"):
        loads[1].wait()
        rowb[...] = route(idb[...])
        loads[3].wait()
        rowf[...] = route(idf[...])
        loads[0].wait()
        loads[2].wait()
        gb[:, 0:1] = norm(saved, gain, normed)
    with scope("barrier"):
        pl.semaphore_wait(barrier, E + 1)
    with scope("rows_b_out"):
        for copy in (hop_b, hop_f, *loads[4:]):
            copy.start()
        dispatch(0, normed, rowb, a1s, a1r)
    with scope("gating_b"):
        colb[...] = stand(rowb[...])
        loads[4].wait()
        score, total, weight = gates(nt(normed[...], router[...]), colb)
        gb[:, 1:2], gb[:, 2:3], gb[:, 3:4] = score[0], score[1], total
        gb[:, 4:5], gb[:, 5:6] = weight[0], weight[1]
    with scope("wait_hop_b"):
        hop_b.wait_recv()
    with scope("cot_near_out"):
        dispatch(1, arr_b, rowb, a2s, a2r)
    with scope("wait_hop_f"):
        hop_f.wait_recv()
    with scope("fwd_near_pack"):
        norm(arr_f, gain, normed)
        dispatch(2, normed, rowf, a3s, a3r)
        colf[...] = stand(rowf[...])
        score, total, weight = gates(nt(normed[...], router[...]), colf)
        gf[:, 0:1], gf[:, 1:2] = weight[0], weight[1]
    with scope("wait_rows_b"):
        for load in loads[5:]:
            load.wait()
        arrive(0, a1s, a1r)
    with scope("gate_up_b"):
        unpack(a1r, xr)

        def gate_up(n, _):
            columns = pl.ds(pl.multiple_of(n * HTILE, HTILE), HTILE)
            gates_b[:, columns] = nn(xr[...], wg[:, columns])
            ups_b[:, columns] = nn(xr[...], wu[:, columns])
            return 0

        lax.fori_loop(0, H // HTILE, gate_up, 0)
    with scope("wait_cot"):
        arrive(1, a2s, a2r)

    def hidden(n, prod):
        columns = pl.ds(pl.multiple_of(n * HTILE, HTILE), HTILE)
        gate, up = gates_b[:, columns], ups_b[:, columns]
        grad = nt(cr[...], wd[columns, :])
        sig = jax.nn.sigmoid(gate)
        act = (gate * sig * up).astype(BF16).astype(F32)
        dg[:, columns] = (grad * up * sig * (1.0 + gate * (1.0 - sig))).astype(BF16)
        du[:, columns] = (grad * gate * sig).astype(BF16)
        return prod + jnp.sum(act * grad, axis=1, keepdims=True)

    with scope("hidden_b"):
        unpack(a2r, cr)
        prod = lax.fori_loop(0, H // HTILE, hidden, jnp.zeros((ROWS, 1), F32))
    prod = jnp.broadcast_to(prod, (ROWS, T)).astype(BF16)
    ps[:, 0:MAIN, :] = prod[0 : E * MAIN].reshape(E, MAIN, T)
    row, lane = iota((E * MAIN, E * OVER), 0), iota((E * MAIN, E * OVER), 1)
    here = (lane == (row // MAIN) * OVER + row % OVER).astype(BF16)
    ps[:, MAIN : 2 * MAIN, :] = nn(here, prod[E * MAIN : ROWS]).astype(BF16).reshape(E, MAIN, T)
    send(3, ps, pr)
    with scope("wait_rows_b_sent"):
        sent(0, a1s, a1r)

    def unit(q, over):
        rows = pl.ds(pl.multiple_of(q * WIDE, 128), WIDE)
        return over + lay(q, a1s, nt(dg[...], wg[rows, :]) + nt(du[...], wu[rows, :]))

    with scope("unit_b"):
        over = lax.fori_loop(0, PARTS, unit, jnp.zeros((E * MAIN, WIDE), F32))
    a1s[:, MAIN * PARTS : BLOCK, :] = over.astype(BF16).reshape(E, MAIN, WIDE)
    send(4, a1s, r1r)

    with scope("wait_rows_f"):
        arrive(2, a3s, a3r)

    def hidden_f(n, _):
        columns = pl.ds(pl.multiple_of(n * HTILE, HTILE), HTILE)
        gate, up = nn(xr[...], wg[:, columns]), nn(xr[...], wu[:, columns])
        dg[:, columns] = (gate * jax.nn.sigmoid(gate) * up).astype(BF16)
        return 0

    with scope("hidden_f"):
        unpack(a3r, xr)
        lax.fori_loop(0, H // HTILE, hidden_f, 0)
    with scope("wait_cot_sent"):
        sent(1, a2s, a2r)

    def down(q, over):
        columns = pl.ds(pl.multiple_of(q * WIDE, 128), WIDE)
        return over + lay(q, a2s, nn(dg[...], wd[:, columns]))

    with scope("down_f"):
        over = lax.fori_loop(0, PARTS, down, jnp.zeros((E * MAIN, WIDE), F32))
    a2s[:, MAIN * PARTS : BLOCK, :] = over.astype(BF16).reshape(E, MAIN, WIDE)
    send(5, a2s, r2r)

    with scope("wait_unit"):
        arrive(3, ps, pr)
        arrive(4, a1s, r1r)
    places = [colb[:, p : p + 1] for p in range(4)]
    score, total = [gb[:, 1:2], gb[:, 2:3]], gb[:, 3:4]
    weight = [gb[:, 4:5], gb[:, 5:6]]
    inv = gb[:, 0:1]
    one = jnp.ones((T, 1), F32)
    product = []
    for k in (0, 1):
        got = nn(spread([places[k]], [one], 0.0), pr[:, 0:MAIN, :].reshape(E * MAIN, T))
        got += nn(spread([places[2 + k]], [one], 0.0), pr[:, MAIN : 2 * MAIN, :].reshape(E * MAIN, T))
        product.append(got[:, 0:1])
    mixed = (product[0] * weight[0] + product[1] * weight[1]) * (1.0 / route_scale)
    lanes = iota((T, E), 1).astype(F32)
    dlogits = jnp.zeros((T, E), F32)
    for k in (0, 1):
        dlogit = route_scale / total * (product[k] - mixed) * score[k] * (1.0 - score[k])
        dlogits += jnp.where(lanes == colb[:, 4 + k : 5 + k], dlogit, 0.0)
    dlogits = dlogits.astype(BF16)
    main_w = spread(places[0:2], weight, 0.0)

    def grad_in(q, dot):
        columns = pl.ds(pl.multiple_of(q * WIDE, 128), WIDE)
        over_w = spread(places[2:4], weight, (OVER * q).astype(F32))
        got = nn(main_w, r1r[:, pl.ds(pl.multiple_of(q * MAIN, MAIN), MAIN), :].reshape(E * MAIN, WIDE))
        got += nn(over_w, r1r[:, MAIN * PARTS : BLOCK, :].reshape(E * MAIN, WIDE))
        got += nn(dlogits, router[:, columns])
        got *= gain[:, columns].astype(F32)
        scaled[:, columns] = got
        return dot + jnp.sum(got * saved[:, columns].astype(F32), axis=1, keepdims=True)

    with scope("finish_b"):
        dot = lax.fori_loop(0, PARTS, grad_in, jnp.zeros((T, 1), F32)) * (1.0 / D)
    back = inv * inv * inv * dot

    def finish_b(q, _):
        columns = pl.ds(pl.multiple_of(q * WIDE, 128), WIDE)
        dx = inv * scaled[:, columns] - saved[:, columns].astype(F32) * back
        saved[:, columns] = (arr_b[:, columns].astype(F32) + dx).astype(BF16)
        return 0

    with scope("finish_b2"):
        lax.fori_loop(0, PARTS, finish_b, 0)
    out_b = pltpu.make_async_copy(saved, ob_hbm, osem.at[0])
    out_b.start()

    places_f = [colf[:, p : p + 1] for p in range(4)]
    weight_f = [gf[:, 0:1], gf[:, 1:2]]
    main_f = spread(places_f[0:2], weight_f, 0.0)
    with scope("wait_out_f"):
        arrive(5, a2s, r2r)

    def finish_f(q, _):
        columns = pl.ds(pl.multiple_of(q * WIDE, 128), WIDE)
        over_w = spread(places_f[2:4], weight_f, (OVER * q).astype(F32))
        got = nn(main_f, r2r[:, pl.ds(pl.multiple_of(q * MAIN, MAIN), MAIN), :].reshape(E * MAIN, WIDE))
        got += nn(over_w, r2r[:, MAIN * PARTS : BLOCK, :].reshape(E * MAIN, WIDE))
        normed[:, columns] = (arr_f[:, columns].astype(F32) + got).astype(BF16)
        return 0

    with scope("finish_f"):
        lax.fori_loop(0, PARTS, finish_f, 0)
    out_f = pltpu.make_async_copy(normed, of_hbm, osem.at[1])
    out_f.start()
    with scope("drain"):
        for copy in (hop_b, hop_f):
            copy.wait_send()
        sent(2, a3s, a3r)
        sent(3, ps, pr)
        sent(4, a1s, r1r)
        sent(5, a2s, r2r)
        out_b.wait()
        out_f.wait()


def leave(f_ref, b_ref, of_ref, ob_ref):
    of_ref[...] = f_ref[...]
    ob_ref[...] = b_ref[...]


def per_device(fwd_acts, bwd_saved, bwd_cot, fwd_ids, bwd_ids, norm_gain, router, w_gate, w_up, w_down):
    def vm(*shape, dtype=BF16):
        return pltpu.VMEM(shape, dtype)

    block = (E, BLOCK, WIDE)
    scratch = [
        vm(D, H), vm(D, H), vm(H, D),
        *[vm(*block) for _ in range(8)],
        vm(E, 2 * MAIN, T), vm(E, 2 * MAIN, T),
        vm(ROWS, D), vm(ROWS, D),
        *[vm(T, D) for _ in range(4)],
        vm(ROWS, H), vm(ROWS, H), vm(ROWS, H, dtype=F32), vm(ROWS, H, dtype=F32),
        vm(T, D, dtype=F32),
        vm(E, D), vm(1, D),
        vm(2, T, dtype=jnp.int32), vm(2, T, dtype=jnp.int32),
        *[vm(8, T, dtype=F32) for _ in range(2)],
        *[vm(T, T, dtype=F32) for _ in range(4)],
        pltpu.SemaphoreType.DMA((6, E)), pltpu.SemaphoreType.DMA((6, E)),
        pltpu.SemaphoreType.DMA((4,)), pltpu.SemaphoreType.DMA((8,)), pltpu.SemaphoreType.DMA((2,)),
    ]
    out = jax.ShapeDtypeStruct((T, D), BF16)
    fwd_out, bwd_grad = pl.pallas_call(
        kernel,
        out_shape=(out, out),
        in_specs=[pl.BlockSpec(memory_space=pl.ANY)] * 10,
        out_specs=(pl.BlockSpec(memory_space=pl.ANY),) * 2,
        scratch_shapes=scratch,
        name="layer",
        compiler_params=pltpu.CompilerParams(
            collective_id=0, has_side_effects=True, vmem_limit_bytes=62 * 1024 * 1024
        ),
        cost_estimate=pl.CostEstimate(flops=8 * 2 * ROWS * D * H, bytes_accessed=30_000_000, transcendentals=0),
    )(
        fwd_acts[0], bwd_saved[0], bwd_cot[0], fwd_ids[0].T, bwd_ids[0].T, norm_gain, router[0].T,
        w_gate[0, 0], w_up[0, 0], w_down[0, 0],
    )
    part = pl.BlockSpec((T // 4, D), lambda i: (i, 0))
    fwd_out, bwd_grad = pl.pallas_call(
        leave,
        out_shape=(out, out),
        grid=(4,),
        in_specs=[part, part],
        out_specs=(part, part),
        name="leave",
        cost_estimate=pl.CostEstimate(flops=0, bytes_accessed=4 * 2 * T * D, transcendentals=0),
    )(fwd_out, bwd_grad)
    return fwd_out[None], bwd_grad[None]


def solution(mesh):
    rows = P("section", "expert", None)
    return jax.shard_map(
        per_device,
        mesh=mesh,
        in_specs=(
            rows, rows, rows, rows, rows, P("section", None), P("section", None, None),
            P("section", "expert", None, None), P("section", "expert", None, None), P("section", "expert", None, None),
        ),
        out_specs=(rows, rows),
        check_vma=False,
    )
```

```python
import functools

import jax
import jax.numpy as jnp
from jax import lax
from jax.experimental import pallas as pl
from jax.experimental.pallas import tpu as pltpu
from jax.sharding import PartitionSpec as P

MESH = pl.DeviceIdType.MESH
F32, BF16 = jnp.float32, jnp.bfloat16
route_scale = 2.5
epsilon = 1e-06

D, H, T, E = 3584, 1024, 128, 16
MAIN, OVER, PARTS = 16, 4, 4
WIDE = D // PARTS
BLOCK = MAIN * PARTS + OVER * PARTS
ROWS = E * (MAIN + OVER)
HALF = E // 2
HTILE = 256
NONE = -1000.0
XS = 4
QUARTER = T // XS


def nt(a, b):
    return lax.dot_general(a, b, (((1,), (1,)), ((), ())), preferred_element_type=F32)


def nn(a, b):
    return jnp.dot(a, b, preferred_element_type=F32)


def iota(shape, axis):
    return lax.broadcasted_iota(jnp.int32, shape, axis)


def route(ids):
    at = iota((E, T), 0)
    hot = [(at == ids[k : k + 1, :]).astype(F32) for k in (0, 1)]
    tri = (iota((T, T), 0) < iota((T, T), 1)).astype(BF16)
    before = nn((hot[0] + hot[1]).astype(BF16), tri)
    line = iota((8, T), 0)
    rows = jnp.zeros((8, T), F32)
    for k in (0, 1):
        slot = jnp.sum(hot[k] * before, axis=0, keepdims=True)
        named = ids[k : k + 1, :].astype(F32)
        base = named * float(MAIN)
        rows = jnp.where(line == k, jnp.where(slot < MAIN, base + slot, NONE), rows)
        rows = jnp.where(line == 2 + k, jnp.where(slot < MAIN, NONE, base + slot - MAIN), rows)
        rows = jnp.where(line == 4 + k, named, rows)
    return rows


def stand(rows):
    return jnp.transpose(jnp.concatenate([rows, jnp.zeros((T - 8, T), F32)], axis=0))


def picks(rows, places, base, shift):
    at = (iota((T, T), 0) + base).astype(F32)
    return sum((at == rows[p : p + 1, :] + shift).astype(F32) for p in places).astype(BF16)


def gates(logits, columns):
    lanes = iota((T, E), 1).astype(F32)
    score = [
        jax.nn.sigmoid(jnp.sum(jnp.where(lanes == columns[:, 4 + k : 5 + k], logits, 0.0), axis=1, keepdims=True))
        for k in (0, 1)
    ]
    total = score[0] + score[1]
    return score, total, [route_scale * s / total for s in score]


def spread(places, values, shift):
    at = iota((T, E * MAIN), 1).astype(F32)
    return sum(jnp.where(at == p + shift, v, 0.0) for p, v in zip(places, values)).astype(BF16)


def kernel(
    fwd_hbm, saved_hbm, cot_hbm, idf_hbm, idb_hbm, gain_hbm, router_hbm, wg_hbm, wu_hbm, wd_hbm,
    of_hbm, ob_hbm,
    wg, wu, wd, a1s, a1r, a2s, a2r, a3s, a3r, r1r, r2r, ps, pr,
    xr, cr, saved, normed, arr_f, arr_b, dg, du, gates_b, ups_b, scaled, router, gain,
    idf, idb, rowf, rowb, colf, colb, gf, gb,
    via, ssem, rsem, hsend, hrecv, vsend, vrecv, lsem, osem,
):
    s, e = lax.axis_index("section"), lax.axis_index("expert")
    layers = lax.axis_size("section")
    after, ahead = (s + 1) % layers, (s + layers - 1) % layers
    yhi, zed, core = e // HALF, e // 2 % 4, e % 2
    near, far = yhi * HALF, (1 - yhi) * HALF

    loads = [
        pltpu.make_async_copy(src, dst, lsem.at[i])
        for i, (src, dst) in enumerate(
            [(saved_hbm, saved), (idb_hbm, idb), (gain_hbm, gain), (idf_hbm, idf),
             (router_hbm, router), (wg_hbm, wg), (wu_hbm, wu), (wd_hbm, wd)]
        )
    ]
    for load in loads[:4]:
        load.start()

    barrier = pltpu.get_barrier_semaphore()

    def greet(d, _):
        pl.semaphore_signal(barrier, inc=1, device_id=(s, (e + d) % E), device_id_type=MESH)
        return 0

    def greet_section(d, _):
        pl.semaphore_signal(barrier, inc=1, device_id=((s + d) % layers, e), device_id_type=MESH)
        return 0

    lax.fori_loop(1, layers, greet_section, 0)
    lax.fori_loop(1, E, greet, 0)

    across, band = s % XS, s // XS
    blocks = ((fwd_hbm, arr_f), (cot_hbm, arr_b))
    ways = ((0, 3, 2, 1), (3, 0, 1, 2))
    towards = (after, ahead)
    at_end = (across == XS - 1, across == 0)

    def quarter(n, j):
        rows = pl.ds(j * QUARTER, QUARTER)
        return pltpu.make_async_remote_copy(
            blocks[n][0].at[rows], blocks[n][1].at[rows], hsend.at[n, j], hrecv.at[n, j],
            device_id=(towards[n], e), device_id_type=MESH)

    def detour(n, j):
        return pltpu.make_async_remote_copy(
            blocks[n][0].at[pl.ds(j * QUARTER, QUARTER)], via.at[n], hsend.at[n, j], vrecv.at[n],
            device_id=((1 - band) * XS + ways[n][j], e), device_id_type=MESH)

    def onward(n, j):
        return pltpu.make_async_remote_copy(
            via.at[n], blocks[n][1].at[pl.ds(j * QUARTER, QUARTER)], vsend.at[n], hrecv.at[n, j],
            device_id=(band * XS + ways[n][0], e), device_id_type=MESH)

    def hop(n):
        quarter(n, 0).start()
        for j in range(1, XS):

            @pl.when(at_end[n])
            def _():
                detour(n, j).start()

            @pl.when(jnp.logical_not(at_end[n]))
            def _():
                quarter(n, j).start()

    def relay(n):
        for j in range(1, XS):

            @pl.when(across == ways[n][j])
            def _():
                detour(n, j).wait_recv()
                onward(n, j).start()

    def hop_arrive(n):
        for j in range(XS):
            quarter(n, j).wait_recv()

    def hop_sent(n):
        for j in range(XS):
            quarter(n, j).wait_send()
        for j in range(1, XS):

            @pl.when(across == ways[n][j])
            def _():
                onward(n, j).wait_send()

    def near_peer(i):
        return near + (zed + i // 2 + 1) % 4 * 2 + (core + i + 1) % 2

    def far_peer(i):
        return far + (zed + 2 + i // 2 * 3) % 4 * 2 + (core + i) % 2

    def near_from(i):
        return near + (zed + 3 - i // 2) % 4 * 2 + (core + i + 1) % 2

    def far_from(i):
        return far + (zed + 2 + i // 2) % 4 * 2 + (core + i) % 2

    def remote(k, src, dst, p, at):
        return pltpu.make_async_remote_copy(
            src.at[p], dst.at[at], ssem.at[k, p], rsem.at[k, at], device_id=(s, p), device_id_type=MESH)

    def own(k, src, dst):
        return pltpu.make_async_copy(src.at[e], dst.at[e], rsem.at[k, e])

    def each(count, act):
        def step(i, _):
            act(i)
            return 0

        lax.fori_loop(0, count, step, 0)

    def send_far(k, src, dst):
        each(HALF, lambda i: remote(k, src, dst, far_peer(i), e).start())

    def send_near(k, src, dst):
        each(HALF - 1, lambda i: remote(k, src, dst, near_peer(i), e).start())
        own(k, src, dst).start()

    def send(k, src, dst):
        send_far(k, src, dst)
        send_near(k, src, dst)

    def arrive(k, src, dst):
        def wait(p):
            remote(k, src, dst, p, p).wait_recv()

        each(HALF - 1, lambda i: wait(near_from(i)))
        each(HALF, lambda i: wait(far_from(i)))
        own(k, src, dst).wait()

    def sent(k, src, dst):
        def wait(p):
            remote(k, src, dst, p, e).wait_send()

        each(HALF - 1, lambda i: wait(near_peer(i)))
        each(HALF, lambda i: wait(far_peer(i)))

    def norm(x_ref, by, out):
        x = x_ref[...].astype(F32)
        inv = lax.rsqrt(jnp.sum(x * x, axis=1, keepdims=True) * (1.0 / D) + epsilon)
        out[...] = (x * inv * by[...].astype(F32)).astype(BF16)
        return inv

    def pack(x_ref, rows, buf, first):
        base = first * MAIN
        main = picks(rows, (0, 1), base, 0.0)

        def step(q, _):
            got = nn(main, x_ref[:, pl.ds(pl.multiple_of(q * WIDE, 128), WIDE)]).astype(BF16)
            buf[pl.ds(first, HALF), pl.ds(pl.multiple_of(q * MAIN, MAIN), MAIN), :] = got.reshape(HALF, MAIN, WIDE)
            return 0

        lax.fori_loop(0, PARTS, step, 0)
        over = sum(
            nn(picks(rows, (2, 3), base, float(OVER * q)), x_ref[:, q * WIDE : (q + 1) * WIDE])
            for q in range(PARTS)
        )
        buf[pl.ds(first, HALF), MAIN * PARTS : BLOCK, :] = over.astype(BF16).reshape(HALF, MAIN, WIDE)

    def dispatch(k, x_ref, rows, src, dst):
        pack(x_ref, rows, src, far)
        send_far(k, src, dst)
        pack(x_ref, rows, src, near)
        send_near(k, src, dst)

    def unpack(buf, out):
        tail = buf[:, MAIN * PARTS : BLOCK, :].reshape(E * MAIN, WIDE)
        row, lane = iota((E * OVER, E * MAIN), 0), iota((E * OVER, E * MAIN), 1)

        def step(q, _):
            columns = pl.ds(pl.multiple_of(q * WIDE, 128), WIDE)
            out[0 : E * MAIN, columns] = buf[:, pl.ds(pl.multiple_of(q * MAIN, MAIN), MAIN), :].reshape(E * MAIN, WIDE)
            pick = (lane == (row // OVER) * MAIN + OVER * q + row % OVER).astype(BF16)
            out[E * MAIN : ROWS, columns] = nn(pick, tail).astype(BF16)
            return 0

        lax.fori_loop(0, PARTS, step, 0)

    def lay(q, buf, value):
        low = value.astype(BF16)
        buf[:, pl.ds(pl.multiple_of(q * MAIN, MAIN), MAIN), :] = low[0 : E * MAIN].reshape(E, MAIN, WIDE)
        row, lane = iota((E * MAIN, E * OVER), 0), iota((E * MAIN, E * OVER), 1)
        here = (lane == (row // MAIN) * OVER + row % OVER) & (row % MAIN // OVER == q)
        return nn(here.astype(BF16), low[E * MAIN : ROWS])

    scope = jax.named_scope
    with scope("start"):
        loads[1].wait()
        rowb[...] = route(idb[...])
        loads[3].wait()
        rowf[...] = route(idf[...])
        loads[0].wait()
        loads[2].wait()
        gb[:, 0:1] = norm(saved, gain, normed)
    with scope("barrier"):
        pl.semaphore_wait(barrier, E - 1 + layers - 1)
    with scope("rows_b_out"):
        hop(1)
        hop(0)
        for load in loads[4:]:
            load.start()
        dispatch(0, normed, rowb, a1s, a1r)
    with scope("gating_b"):
        colb[...] = stand(rowb[...])
        loads[4].wait()
        score, total, weight = gates(nt(normed[...], router[...]), colb)
        gb[:, 1:2], gb[:, 2:3], gb[:, 3:4] = score[0], score[1], total
        gb[:, 4:5], gb[:, 5:6] = weight[0], weight[1]
    with scope("relay"):
        relay(1)
        relay(0)
    with scope("wait_hop_b"):
        hop_arrive(1)
    with scope("cot_near_out"):
        dispatch(1, arr_b, rowb, a2s, a2r)
    with scope("wait_hop_f"):
        hop_arrive(0)
    with scope("fwd_near_pack"):
        norm(arr_f, gain, normed)
        dispatch(2, normed, rowf, a3s, a3r)
        colf[...] = stand(rowf[...])
        score, total, weight = gates(nt(normed[...], router[...]), colf)
        gf[:, 0:1], gf[:, 1:2] = weight[0], weight[1]
    with scope("wait_rows_b"):
        for load in loads[5:]:
            load.wait()
        arrive(0, a1s, a1r)
    with scope("gate_up_b"):
        unpack(a1r, xr)

        def gate_up(n, _):
            columns = pl.ds(pl.multiple_of(n * HTILE, HTILE), HTILE)
            gates_b[:, columns] = nn(xr[...], wg[:, columns])
            ups_b[:, columns] = nn(xr[...], wu[:, columns])
            return 0

        lax.fori_loop(0, H // HTILE, gate_up, 0)
    with scope("wait_cot"):
        arrive(1, a2s, a2r)

    def hidden(n, prod):
        columns = pl.ds(pl.multiple_of(n * HTILE, HTILE), HTILE)
        gate, up = gates_b[:, columns], ups_b[:, columns]
        grad = nt(cr[...], wd[columns, :])
        sig = jax.nn.sigmoid(gate)
        act = (gate * sig * up).astype(BF16).astype(F32)
        dg[:, columns] = (grad * up * sig * (1.0 + gate * (1.0 - sig))).astype(BF16)
        du[:, columns] = (grad * gate * sig).astype(BF16)
        return prod + jnp.sum(act * grad, axis=1, keepdims=True)

    with scope("hidden_b"):
        unpack(a2r, cr)
        prod = lax.fori_loop(0, H // HTILE, hidden, jnp.zeros((ROWS, 1), F32))
    prod = jnp.broadcast_to(prod, (ROWS, T)).astype(BF16)
    ps[:, 0:MAIN, :] = prod[0 : E * MAIN].reshape(E, MAIN, T)
    row, lane = iota((E * MAIN, E * OVER), 0), iota((E * MAIN, E * OVER), 1)
    here = (lane == (row // MAIN) * OVER + row % OVER).astype(BF16)
    ps[:, MAIN : 2 * MAIN, :] = nn(here, prod[E * MAIN : ROWS]).astype(BF16).reshape(E, MAIN, T)
    send(3, ps, pr)
    with scope("wait_rows_b_sent"):
        sent(0, a1s, a1r)

    def unit(q, over):
        rows = pl.ds(pl.multiple_of(q * WIDE, 128), WIDE)
        return over + lay(q, a1s, nt(dg[...], wg[rows, :]) + nt(du[...], wu[rows, :]))

    with scope("unit_b"):
        over = lax.fori_loop(0, PARTS, unit, jnp.zeros((E * MAIN, WIDE), F32))
    a1s[:, MAIN * PARTS : BLOCK, :] = over.astype(BF16).reshape(E, MAIN, WIDE)
    send(4, a1s, r1r)

    with scope("wait_rows_f"):
        arrive(2, a3s, a3r)

    def hidden_f(n, _):
        columns = pl.ds(pl.multiple_of(n * HTILE, HTILE), HTILE)
        gate, up = nn(xr[...], wg[:, columns]), nn(xr[...], wu[:, columns])
        dg[:, columns] = (gate * jax.nn.sigmoid(gate) * up).astype(BF16)
        return 0

    with scope("hidden_f"):
        unpack(a3r, xr)
        lax.fori_loop(0, H // HTILE, hidden_f, 0)
    with scope("wait_cot_sent"):
        sent(1, a2s, a2r)

    def down(q, over):
        columns = pl.ds(pl.multiple_of(q * WIDE, 128), WIDE)
        return over + lay(q, a2s, nn(dg[...], wd[:, columns]))

    with scope("down_f"):
        over = lax.fori_loop(0, PARTS, down, jnp.zeros((E * MAIN, WIDE), F32))
    a2s[:, MAIN * PARTS : BLOCK, :] = over.astype(BF16).reshape(E, MAIN, WIDE)
    send(5, a2s, r2r)

    with scope("wait_unit"):
        arrive(3, ps, pr)
        arrive(4, a1s, r1r)
    places = [colb[:, p : p + 1] for p in range(4)]
    score, total = [gb[:, 1:2], gb[:, 2:3]], gb[:, 3:4]
    weight = [gb[:, 4:5], gb[:, 5:6]]
    inv = gb[:, 0:1]
    one = jnp.ones((T, 1), F32)
    product = []
    for k in (0, 1):
        got = nn(spread([places[k]], [one], 0.0), pr[:, 0:MAIN, :].reshape(E * MAIN, T))
        got += nn(spread([places[2 + k]], [one], 0.0), pr[:, MAIN : 2 * MAIN, :].reshape(E * MAIN, T))
        product.append(got[:, 0:1])
    mixed = (product[0] * weight[0] + product[1] * weight[1]) * (1.0 / route_scale)
    lanes = iota((T, E), 1).astype(F32)
    dlogits = jnp.zeros((T, E), F32)
    for k in (0, 1):
        dlogit = route_scale / total * (product[k] - mixed) * score[k] * (1.0 - score[k])
        dlogits += jnp.where(lanes == colb[:, 4 + k : 5 + k], dlogit, 0.0)
    dlogits = dlogits.astype(BF16)
    main_w = spread(places[0:2], weight, 0.0)

    def grad_in(q, dot):
        columns = pl.ds(pl.multiple_of(q * WIDE, 128), WIDE)
        over_w = spread(places[2:4], weight, (OVER * q).astype(F32))
        got = nn(main_w, r1r[:, pl.ds(pl.multiple_of(q * MAIN, MAIN), MAIN), :].reshape(E * MAIN, WIDE))
        got += nn(over_w, r1r[:, MAIN * PARTS : BLOCK, :].reshape(E * MAIN, WIDE))
        got += nn(dlogits, router[:, columns])
        got *= gain[:, columns].astype(F32)
        scaled[:, columns] = got
        return dot + jnp.sum(got * saved[:, columns].astype(F32), axis=1, keepdims=True)

    with scope("finish_b"):
        dot = lax.fori_loop(0, PARTS, grad_in, jnp.zeros((T, 1), F32)) * (1.0 / D)
    back = inv * inv * inv * dot

    def finish_b(q, _):
        columns = pl.ds(pl.multiple_of(q * WIDE, 128), WIDE)
        dx = inv * scaled[:, columns] - saved[:, columns].astype(F32) * back
        saved[:, columns] = (arr_b[:, columns].astype(F32) + dx).astype(BF16)
        return 0

    with scope("finish_b2"):
        lax.fori_loop(0, PARTS, finish_b, 0)
    out_b = pltpu.make_async_copy(saved, ob_hbm, osem.at[0])
    out_b.start()

    places_f = [colf[:, p : p + 1] for p in range(4)]
    weight_f = [gf[:, 0:1], gf[:, 1:2]]
    main_f = spread(places_f[0:2], weight_f, 0.0)
    with scope("wait_out_f"):
        arrive(5, a2s, r2r)

    def finish_f(q, _):
        columns = pl.ds(pl.multiple_of(q * WIDE, 128), WIDE)
        over_w = spread(places_f[2:4], weight_f, (OVER * q).astype(F32))
        got = nn(main_f, r2r[:, pl.ds(pl.multiple_of(q * MAIN, MAIN), MAIN), :].reshape(E * MAIN, WIDE))
        got += nn(over_w, r2r[:, MAIN * PARTS : BLOCK, :].reshape(E * MAIN, WIDE))
        normed[:, columns] = (arr_f[:, columns].astype(F32) + got).astype(BF16)
        return 0

    with scope("finish_f"):
        lax.fori_loop(0, PARTS, finish_f, 0)
    out_f = pltpu.make_async_copy(normed, of_hbm, osem.at[1])
    out_f.start()
    with scope("drain"):
        hop_sent(0)
        hop_sent(1)
        sent(2, a3s, a3r)
        sent(3, ps, pr)
        sent(4, a1s, r1r)
        sent(5, a2s, r2r)
        out_b.wait()
        out_f.wait()


def leave(f_hbm, b_hbm, of_hbm, ob_hbm, f_ref, b_ref, in_sem, out_sem):
    pairs = []
    for i, (src, mid, dst) in enumerate(((f_hbm, f_ref, of_hbm), (b_hbm, b_ref, ob_hbm))):
        for j in range(4):
            part = pl.ds(j * (T // 4), T // 4)
            pairs.append(
                (pltpu.make_async_copy(src.at[part], mid.at[part], in_sem.at[i, j]),
                 pltpu.make_async_copy(mid.at[part], dst.at[part], out_sem.at[i, j]))
            )
    for come, _ in pairs:
        come.start()
    for come, go in pairs:
        come.wait()
        go.start()
    for _, go in pairs:
        go.wait()


def per_device(fwd_acts, bwd_saved, bwd_cot, fwd_ids, bwd_ids, norm_gain, router, w_gate, w_up, w_down):
    def vm(*shape, dtype=BF16):
        return pltpu.VMEM(shape, dtype)

    block = (E, BLOCK, WIDE)
    scratch = [
        vm(D, H), vm(D, H), vm(H, D),
        *[vm(*block) for _ in range(8)],
        vm(E, 2 * MAIN, T), vm(E, 2 * MAIN, T),
        vm(ROWS, D), vm(ROWS, D),
        *[vm(T, D) for _ in range(4)],
        vm(ROWS, H), vm(ROWS, H), vm(ROWS, H, dtype=F32), vm(ROWS, H, dtype=F32),
        vm(T, D, dtype=F32),
        vm(E, D), vm(1, D),
        vm(2, T, dtype=jnp.int32), vm(2, T, dtype=jnp.int32),
        *[vm(8, T, dtype=F32) for _ in range(2)],
        *[vm(T, T, dtype=F32) for _ in range(4)],
        vm(2, QUARTER, D),
        pltpu.SemaphoreType.DMA((6, E)), pltpu.SemaphoreType.DMA((6, E)),
        pltpu.SemaphoreType.DMA((2, XS)), pltpu.SemaphoreType.DMA((2, XS)),
        pltpu.SemaphoreType.DMA((2,)), pltpu.SemaphoreType.DMA((2,)),
        pltpu.SemaphoreType.DMA((8,)), pltpu.SemaphoreType.DMA((2,)),
    ]
    out = jax.ShapeDtypeStruct((T, D), BF16)
    fwd_out, bwd_grad = pl.pallas_call(
        kernel,
        out_shape=(out, out),
        in_specs=[pl.BlockSpec(memory_space=pl.ANY)] * 10,
        out_specs=(pl.BlockSpec(memory_space=pl.ANY),) * 2,
        scratch_shapes=scratch,
        name="layer",
        compiler_params=pltpu.CompilerParams(
            collective_id=0, has_side_effects=True, vmem_limit_bytes=62 * 1024 * 1024
        ),
        cost_estimate=pl.CostEstimate(flops=8 * 2 * ROWS * D * H, bytes_accessed=30_000_000, transcendentals=0),
    )(
        fwd_acts[0], bwd_saved[0], bwd_cot[0], fwd_ids[0].T, bwd_ids[0].T, norm_gain, router[0].T,
        w_gate[0, 0], w_up[0, 0], w_down[0, 0],
    )
    fwd_out, bwd_grad = pl.pallas_call(
        leave,
        out_shape=(out, out),
        in_specs=[pl.BlockSpec(memory_space=pl.ANY)] * 2,
        out_specs=(pl.BlockSpec(memory_space=pl.ANY),) * 2,
        scratch_shapes=[vm(T, D), vm(T, D), pltpu.SemaphoreType.DMA((2, 4)), pltpu.SemaphoreType.DMA((2, 4))],
        name="leave",
        cost_estimate=pl.CostEstimate(flops=0, bytes_accessed=4 * 2 * T * D, transcendentals=0),
    )(fwd_out, bwd_grad)
    return fwd_out[None], bwd_grad[None]


def solution(mesh):
    rows = P("section", "expert", None)
    return jax.shard_map(
        per_device,
        mesh=mesh,
        in_specs=(
            rows, rows, rows, rows, rows, P("section", None), P("section", None, None),
            P("section", "expert", None, None), P("section", "expert", None, None), P("section", "expert", None, None),
        ),
        out_specs=(rows, rows),
        check_vma=False,
    )
```

```python
import functools

import jax
import jax.numpy as jnp
from jax import lax
from jax.experimental import pallas as pl
from jax.experimental.pallas import tpu as pltpu
from jax.sharding import PartitionSpec as P

MESH = pl.DeviceIdType.MESH
F32, BF16 = jnp.float32, jnp.bfloat16
route_scale = 2.5
epsilon = 1e-06

D, H, T, E = 3584, 1024, 128, 16
MAIN, OVER, PARTS = 16, 4, 4
WIDE = D // PARTS
BLOCK = MAIN * PARTS + OVER * PARTS
ROWS = E * (MAIN + OVER)
HALF = E // 2
HTILE = 256
NONE = -1000.0
XS = 4
QUARTER = T // XS
TURNS = (1, 3, 2, 0)
SPANS = {5: (0, 3 * MAIN), 6: (3 * MAIN, 2 * MAIN)}


def nt(a, b):
    return lax.dot_general(a, b, (((1,), (1,)), ((), ())), preferred_element_type=F32)


def nn(a, b):
    return jnp.dot(a, b, preferred_element_type=F32)


def iota(shape, axis):
    return lax.broadcasted_iota(jnp.int32, shape, axis)


def route(ids):
    at = iota((E, T), 0)
    hot = [(at == ids[k : k + 1, :]).astype(F32) for k in (0, 1)]
    tri = (iota((T, T), 0) < iota((T, T), 1)).astype(BF16)
    before = nn((hot[0] + hot[1]).astype(BF16), tri)
    line = iota((8, T), 0)
    rows = jnp.zeros((8, T), F32)
    for k in (0, 1):
        slot = jnp.sum(hot[k] * before, axis=0, keepdims=True)
        named = ids[k : k + 1, :].astype(F32)
        base = named * float(MAIN)
        rows = jnp.where(line == k, jnp.where(slot < MAIN, base + slot, NONE), rows)
        rows = jnp.where(line == 2 + k, jnp.where(slot < MAIN, NONE, base + slot - MAIN), rows)
        rows = jnp.where(line == 4 + k, named, rows)
    return rows


def stand(rows):
    return jnp.transpose(jnp.concatenate([rows, jnp.zeros((T - 8, T), F32)], axis=0))


def picks(rows, places, base, shift):
    at = (iota((T, T), 0) + base).astype(F32)
    return sum((at == rows[p : p + 1, :] + shift).astype(F32) for p in places).astype(BF16)


def gates(logits, columns):
    lanes = iota((T, E), 1).astype(F32)
    score = [
        jax.nn.sigmoid(jnp.sum(jnp.where(lanes == columns[:, 4 + k : 5 + k], logits, 0.0), axis=1, keepdims=True))
        for k in (0, 1)
    ]
    total = score[0] + score[1]
    return score, total, [route_scale * s / total for s in score]


def spread(places, values, shift):
    at = iota((T, E * MAIN), 1).astype(F32)
    return sum(jnp.where(at == p + shift, v, 0.0) for p, v in zip(places, values)).astype(BF16)


def kernel(
    fwd_hbm, saved_hbm, cot_hbm, idf_hbm, idb_hbm, gain_hbm, router_hbm, wg_hbm, wu_hbm, wd_hbm,
    of_hbm, ob_hbm,
    wg, wu, wd, a1s, a1r, a2s, a2r, a3s, a3r, r1r, r2r, ps, pr,
    xr, saved, normed, arr_f, arr_b, dg, du, gates_b, ups_b, scaled, router, gain,
    idf, idb, rowf, rowb, colf, colb, gf, gb,
    via, ssem, rsem, hsend, hrecv, vsend, vrecv, lsem, osem,
):
    s, e = lax.axis_index("section"), lax.axis_index("expert")
    layers = lax.axis_size("section")
    after, ahead = (s + 1) % layers, (s + layers - 1) % layers
    yhi, zed, core = e // HALF, e // 2 % 4, e % 2
    near, far = yhi * HALF, (1 - yhi) * HALF

    loads = [
        pltpu.make_async_copy(src, dst, lsem.at[i])
        for i, (src, dst) in enumerate(
            [(saved_hbm, saved), (idb_hbm, idb), (gain_hbm, gain), (idf_hbm, idf),
             (router_hbm, router), (wg_hbm, wg), (wu_hbm, wu), (wd_hbm, wd)]
        )
    ]
    for load in loads[:4]:
        load.start()

    barrier = pltpu.get_barrier_semaphore()

    def greet(d, _):
        pl.semaphore_signal(barrier, inc=1, device_id=(s, (e + d) % E), device_id_type=MESH)
        return 0

    def greet_section(d, _):
        pl.semaphore_signal(barrier, inc=1, device_id=((s + d) % layers, e), device_id_type=MESH)
        return 0

    lax.fori_loop(1, layers, greet_section, 0)
    lax.fori_loop(1, E, greet, 0)

    across, band = s % XS, s // XS
    blocks = ((fwd_hbm, arr_f), (cot_hbm, arr_b))
    ways = ((0, 3, 2, 1), (3, 0, 1, 2))
    towards = (after, ahead)
    at_end = (across == XS - 1, across == 0)

    def quarter(n, j):
        rows = pl.ds(j * QUARTER, QUARTER)
        return pltpu.make_async_remote_copy(
            blocks[n][0].at[rows], blocks[n][1].at[rows], hsend.at[n, j], hrecv.at[n, j],
            device_id=(towards[n], e), device_id_type=MESH)

    def detour(n, j):
        return pltpu.make_async_remote_copy(
            blocks[n][0].at[pl.ds(j * QUARTER, QUARTER)], via.at[n], hsend.at[n, j], vrecv.at[n],
            device_id=((1 - band) * XS + ways[n][j], e), device_id_type=MESH)

    def onward(n, j):
        return pltpu.make_async_remote_copy(
            via.at[n], blocks[n][1].at[pl.ds(j * QUARTER, QUARTER)], vsend.at[n], hrecv.at[n, j],
            device_id=(band * XS + ways[n][0], e), device_id_type=MESH)

    def hop(n):
        quarter(n, 0).start()
        for j in range(1, XS):

            @pl.when(at_end[n])
            def _():
                detour(n, j).start()

            @pl.when(jnp.logical_not(at_end[n]))
            def _():
                quarter(n, j).start()

    def relay(n):
        for j in range(1, XS):

            @pl.when(across == ways[n][j])
            def _():
                detour(n, j).wait_recv()
                onward(n, j).start()

    def hop_arrive(n):
        for j in range(XS):
            quarter(n, j).wait_recv()

    def hop_sent(n):
        for j in range(XS):
            quarter(n, j).wait_send()
        for j in range(1, XS):

            @pl.when(across == ways[n][j])
            def _():
                onward(n, j).wait_send()

    def peer(half, dz, dc):
        return half + (zed + dz) % 4 * 2 + (core + dc) % 2

    def remote(k, src, dst, p, at):
        first, count = SPANS.get(k, (0, src.shape[1]))
        span = pl.ds(first, count)
        return pltpu.make_async_remote_copy(
            src.at[p, span], dst.at[at, span], ssem.at[k, p], rsem.at[k, at], device_id=(s, p), device_id_type=MESH)

    def own(k, src, dst):
        first, count = SPANS.get(k, (0, src.shape[1]))
        span = pl.ds(first, count)
        return pltpu.make_async_copy(src.at[e, span], dst.at[e, span], rsem.at[k, e])

    def others(act):
        def step(d, _):
            act((e + d) % E)
            return 0

        lax.fori_loop(1, E, step, 0)

    def send_far(k, src, dst):
        for dc in (0, 1):
            for dz in TURNS:
                remote(k, src, dst, peer(far, dz, dc), e).start()

    def send_near(k, src, dst):
        for dc in (1, 0):
            for dz in TURNS:
                if (dz, dc) != (0, 0):
                    remote(k, src, dst, peer(near, dz, dc), e).start()
        own(k, src, dst).start()

    def send(k, src, dst):
        send_far(k, src, dst)
        send_near(k, src, dst)

    def arrive(k, src, dst):
        others(lambda p: remote(k, src, dst, p, p).wait_recv())
        own(k, src, dst).wait()

    def sent(k, src, dst):
        others(lambda p: remote(k, src, dst, p, e).wait_send())

    def norm(x_ref, by, out):
        x = x_ref[...].astype(F32)
        inv = lax.rsqrt(jnp.sum(x * x, axis=1, keepdims=True) * (1.0 / D) + epsilon)
        out[...] = (x * inv * by[...].astype(F32)).astype(BF16)
        return inv

    def pack(x_ref, rows, buf, first):
        base = first * MAIN
        main = picks(rows, (0, 1), base, 0.0)

        def step(q, _):
            got = nn(main, x_ref[:, pl.ds(pl.multiple_of(q * WIDE, 128), WIDE)]).astype(BF16)
            buf[pl.ds(first, HALF), pl.ds(pl.multiple_of(q * MAIN + MAIN, MAIN), MAIN), :] = got.reshape(HALF, MAIN, WIDE)
            return 0

        lax.fori_loop(0, PARTS, step, 0)
        over = sum(
            nn(picks(rows, (2, 3), base, float(OVER * q)), x_ref[:, q * WIDE : (q + 1) * WIDE])
            for q in range(PARTS)
        )
        buf[pl.ds(first, HALF), 0:MAIN, :] = over.astype(BF16).reshape(HALF, MAIN, WIDE)

    def dispatch(k, x_ref, rows, src, dst):
        pack(x_ref, rows, src, far)
        send_far(k, src, dst)
        pack(x_ref, rows, src, near)
        send_near(k, src, dst)

    def unpack(buf, out):
        tail = buf[:, 0:MAIN, :].reshape(E * MAIN, WIDE)
        row, lane = iota((E * OVER, E * MAIN), 0), iota((E * OVER, E * MAIN), 1)

        def step(q, _):
            columns = pl.ds(pl.multiple_of(q * WIDE, 128), WIDE)
            out[0 : E * MAIN, columns] = buf[:, pl.ds(pl.multiple_of(q * MAIN + MAIN, MAIN), MAIN), :].reshape(E * MAIN, WIDE)
            pick = (lane == (row // OVER) * MAIN + OVER * q + row % OVER).astype(BF16)
            out[E * MAIN : ROWS, columns] = nn(pick, tail).astype(BF16)
            return 0

        lax.fori_loop(0, PARTS, step, 0)

    def lay(q, buf, value):
        low = value.astype(BF16)
        buf[:, pl.ds(pl.multiple_of(q * MAIN + MAIN, MAIN), MAIN), :] = low[0 : E * MAIN].reshape(E, MAIN, WIDE)
        row, lane = iota((E * MAIN, E * OVER), 0), iota((E * MAIN, E * OVER), 1)
        here = (lane == (row // MAIN) * OVER + row % OVER) & (row % MAIN // OVER == q)
        return nn(here.astype(BF16), low[E * MAIN : ROWS])

    scope = jax.named_scope
    with scope("barrier"):
        pl.semaphore_wait(barrier, E - 1 + layers - 1)
        hop(1)
        hop(0)
        for load in loads[4:]:
            load.start()
    with scope("start"):
        loads[1].wait()
        rowb[...] = route(idb[...])
        loads[0].wait()
        loads[2].wait()
        gb[:, 0:1] = norm(saved, gain, normed)
    with scope("rows_b_out"):
        dispatch(0, normed, rowb, a1s, a1r)
    with scope("gating_b"):
        colb[...] = stand(rowb[...])
        loads[4].wait()
        score, total, weight = gates(nt(normed[...], router[...]), colb)
        gb[:, 1:2], gb[:, 2:3], gb[:, 3:4] = score[0], score[1], total
        gb[:, 4:5], gb[:, 5:6] = weight[0], weight[1]
        loads[3].wait()
        rowf[...] = route(idf[...])
    with scope("relay"):
        relay(1)
        relay(0)
    with scope("wait_hop_b"):
        hop_arrive(1)
    with scope("cot_near_out"):
        dispatch(1, arr_b, rowb, a2s, a2r)
    with scope("wait_hop_f"):
        hop_arrive(0)
    with scope("fwd_near_pack"):
        norm(arr_f, gain, normed)
        dispatch(2, normed, rowf, a3s, a3r)
        colf[...] = stand(rowf[...])
        score, total, weight = gates(nt(normed[...], router[...]), colf)
        gf[:, 0:1], gf[:, 1:2] = weight[0], weight[1]
    with scope("wait_rows_b"):
        for load in loads[5:]:
            load.wait()
        arrive(0, a1s, a1r)
    with scope("gate_up_b"):
        unpack(a1r, xr)

        def gate_up(n, _):
            columns = pl.ds(pl.multiple_of(n * HTILE, HTILE), HTILE)
            gates_b[:, columns] = nn(xr[...], wg[:, columns])
            ups_b[:, columns] = nn(xr[...], wu[:, columns])
            return 0

        lax.fori_loop(0, H // HTILE, gate_up, 0)
    with scope("wait_cot"):
        arrive(1, a2s, a2r)

    def hidden(n, prod):
        columns = pl.ds(pl.multiple_of(n * HTILE, HTILE), HTILE)
        gate, up = gates_b[:, columns], ups_b[:, columns]
        grad = nt(xr[...], wd[columns, :])
        sig = jax.nn.sigmoid(gate)
        act = (gate * sig * up).astype(BF16).astype(F32)
        dg[:, columns] = (grad * up * sig * (1.0 + gate * (1.0 - sig))).astype(BF16)
        du[:, columns] = (grad * gate * sig).astype(BF16)
        return prod + jnp.sum(act * grad, axis=1, keepdims=True)

    with scope("hidden_b"):
        unpack(a2r, xr)
        prod = lax.fori_loop(0, H // HTILE, hidden, jnp.zeros((ROWS, 1), F32))
    prod = jnp.broadcast_to(prod, (ROWS, T)).astype(BF16)
    ps[:, 0:MAIN, :] = prod[0 : E * MAIN].reshape(E, MAIN, T)
    row, lane = iota((E * MAIN, E * OVER), 0), iota((E * MAIN, E * OVER), 1)
    here = (lane == (row // MAIN) * OVER + row % OVER).astype(BF16)
    ps[:, MAIN : 2 * MAIN, :] = nn(here, prod[E * MAIN : ROWS]).astype(BF16).reshape(E, MAIN, T)
    send(3, ps, pr)
    with scope("wait_rows_b_sent"):
        sent(0, a1s, a1r)

    def unit(q, over):
        rows = pl.ds(pl.multiple_of(q * WIDE, 128), WIDE)
        return over + lay(q, a1s, nt(dg[...], wg[rows, :]) + nt(du[...], wu[rows, :]))

    with scope("unit_b"):
        over = lax.fori_loop(0, PARTS, unit, jnp.zeros((E * MAIN, WIDE), F32))
    a1s[:, 0:MAIN, :] = over.astype(BF16).reshape(E, MAIN, WIDE)
    send(4, a1s, r1r)

    with scope("wait_rows_f"):
        arrive(2, a3s, a3r)

    def hidden_f(n, _):
        columns = pl.ds(pl.multiple_of(n * HTILE, HTILE), HTILE)
        gate, up = nn(xr[...], wg[:, columns]), nn(xr[...], wu[:, columns])
        dg[:, columns] = (gate * jax.nn.sigmoid(gate) * up).astype(BF16)
        return 0

    with scope("hidden_f"):
        unpack(a3r, xr)
        lax.fori_loop(0, H // HTILE, hidden_f, 0)
    with scope("wait_cot_sent"):
        sent(1, a2s, a2r)

    def down(q, over):
        columns = pl.ds(pl.multiple_of(q * WIDE, 128), WIDE)
        return over + lay(q, a2s, nn(dg[...], wd[:, columns]))

    with scope("down_f"):
        over = lax.fori_loop(0, PARTS, down, jnp.zeros((E * MAIN, WIDE), F32))
    a2s[:, 0:MAIN, :] = over.astype(BF16).reshape(E, MAIN, WIDE)
    send(5, a2s, r2r)
    send(6, a2s, r2r)

    with scope("wait_unit"):
        arrive(3, ps, pr)
        arrive(4, a1s, r1r)
    places = [colb[:, p : p + 1] for p in range(4)]
    score, total = [gb[:, 1:2], gb[:, 2:3]], gb[:, 3:4]
    weight = [gb[:, 4:5], gb[:, 5:6]]
    inv = gb[:, 0:1]
    one = jnp.ones((T, 1), F32)
    product = []
    for k in (0, 1):
        got = nn(spread([places[k]], [one], 0.0), pr[:, 0:MAIN, :].reshape(E * MAIN, T))
        got += nn(spread([places[2 + k]], [one], 0.0), pr[:, MAIN : 2 * MAIN, :].reshape(E * MAIN, T))
        product.append(got[:, 0:1])
    mixed = (product[0] * weight[0] + product[1] * weight[1]) * (1.0 / route_scale)
    lanes = iota((T, E), 1).astype(F32)
    dlogits = jnp.zeros((T, E), F32)
    for k in (0, 1):
        dlogit = route_scale / total * (product[k] - mixed) * score[k] * (1.0 - score[k])
        dlogits += jnp.where(lanes == colb[:, 4 + k : 5 + k], dlogit, 0.0)
    dlogits = dlogits.astype(BF16)
    main_w = spread(places[0:2], weight, 0.0)

    def grad_in(q, dot):
        columns = pl.ds(pl.multiple_of(q * WIDE, 128), WIDE)
        over_w = spread(places[2:4], weight, (OVER * q).astype(F32))
        got = nn(main_w, r1r[:, pl.ds(pl.multiple_of(q * MAIN + MAIN, MAIN), MAIN), :].reshape(E * MAIN, WIDE))
        got += nn(over_w, r1r[:, 0:MAIN, :].reshape(E * MAIN, WIDE))
        got += nn(dlogits, router[:, columns])
        got *= gain[:, columns].astype(F32)
        scaled[:, columns] = got
        return dot + jnp.sum(got * saved[:, columns].astype(F32), axis=1, keepdims=True)

    with scope("finish_b"):
        dot = lax.fori_loop(0, PARTS, grad_in, jnp.zeros((T, 1), F32)) * (1.0 / D)
    back = inv * inv * inv * dot

    def finish_b(q, _):
        columns = pl.ds(pl.multiple_of(q * WIDE, 128), WIDE)
        dx = inv * scaled[:, columns] - saved[:, columns].astype(F32) * back
        saved[:, columns] = (arr_b[:, columns].astype(F32) + dx).astype(BF16)
        return 0

    with scope("finish_b2"):
        lax.fori_loop(0, PARTS, finish_b, 0)
    out_b = pltpu.make_async_copy(saved, ob_hbm, osem.at[0])
    out_b.start()
    halves = [pl.ds(i * (D // 2), D // 2) for i in (0, 1)]
    out_f = [pltpu.make_async_copy(normed.at[:, half], of_hbm.at[:, half], osem.at[1 + i]) for i, half in enumerate(halves)]

    places_f = [colf[:, p : p + 1] for p in range(4)]
    weight_f = [gf[:, 0:1], gf[:, 1:2]]
    main_f = spread(places_f[0:2], weight_f, 0.0)
    def finish_f(q, _):
        columns = pl.ds(pl.multiple_of(q * WIDE, 128), WIDE)
        over_w = spread(places_f[2:4], weight_f, (OVER * q).astype(F32))
        got = nn(main_f, r2r[:, pl.ds(pl.multiple_of(q * MAIN + MAIN, MAIN), MAIN), :].reshape(E * MAIN, WIDE))
        got += nn(over_w, r2r[:, 0:MAIN, :].reshape(E * MAIN, WIDE))
        normed[:, columns] = (arr_f[:, columns].astype(F32) + got).astype(BF16)
        return 0

    with scope("finish_f"):
        arrive(5, a2s, r2r)
        lax.fori_loop(0, PARTS // 2, finish_f, 0)
        out_f[0].start()
        arrive(6, a2s, r2r)
        lax.fori_loop(PARTS // 2, PARTS, finish_f, 0)
        out_f[1].start()
    with scope("drain"):
        hop_sent(0)
        hop_sent(1)
        sent(2, a3s, a3r)
        sent(3, ps, pr)
        sent(4, a1s, r1r)
        sent(5, a2s, r2r)
        sent(6, a2s, r2r)
        out_b.wait()
        out_f[0].wait()
        out_f[1].wait()


def leave(f_hbm, b_hbm, of_hbm, ob_hbm, f_ref, b_ref, in_sem, out_sem):
    pairs = []
    for i, (src, mid, dst) in enumerate(((f_hbm, f_ref, of_hbm), (b_hbm, b_ref, ob_hbm))):
        for j in range(4):
            part = pl.ds(j * (T // 4), T // 4)
            pairs.append(
                (pltpu.make_async_copy(src.at[part], mid.at[part], in_sem.at[i, j]),
                 pltpu.make_async_copy(mid.at[part], dst.at[part], out_sem.at[i, j]))
            )
    for come, _ in pairs:
        come.start()
    for come, go in pairs:
        come.wait()
        go.start()
    for _, go in pairs:
        go.wait()


def per_device(fwd_acts, bwd_saved, bwd_cot, fwd_ids, bwd_ids, norm_gain, router, w_gate, w_up, w_down):
    def vm(*shape, dtype=BF16):
        return pltpu.VMEM(shape, dtype)

    block = (E, BLOCK, WIDE)
    scratch = [
        vm(D, H), vm(D, H), vm(H, D),
        *[vm(*block) for _ in range(8)],
        vm(E, 2 * MAIN, T), vm(E, 2 * MAIN, T),
        vm(ROWS, D),
        *[vm(T, D) for _ in range(4)],
        vm(ROWS, H), vm(ROWS, H), vm(ROWS, H, dtype=F32), vm(ROWS, H, dtype=F32),
        vm(T, D, dtype=F32),
        vm(E, D), vm(1, D),
        vm(2, T, dtype=jnp.int32), vm(2, T, dtype=jnp.int32),
        *[vm(8, T, dtype=F32) for _ in range(2)],
        *[vm(T, T, dtype=F32) for _ in range(4)],
        vm(2, QUARTER, D),
        pltpu.SemaphoreType.DMA((7, E)), pltpu.SemaphoreType.DMA((7, E)),
        pltpu.SemaphoreType.DMA((2, XS)), pltpu.SemaphoreType.DMA((2, XS)),
        pltpu.SemaphoreType.DMA((2,)), pltpu.SemaphoreType.DMA((2,)),
        pltpu.SemaphoreType.DMA((8,)), pltpu.SemaphoreType.DMA((3,)),
    ]
    out = jax.ShapeDtypeStruct((T, D), BF16)
    fwd_out, bwd_grad = pl.pallas_call(
        kernel,
        out_shape=(out, out),
        in_specs=[pl.BlockSpec(memory_space=pltpu.HBM)] * 10,
        out_specs=(pl.BlockSpec(memory_space=pltpu.HBM),) * 2,
        scratch_shapes=scratch,
        name="layer",
        compiler_params=pltpu.CompilerParams(
            collective_id=0, has_side_effects=True, vmem_limit_bytes=62 * 1024 * 1024
        ),
        cost_estimate=pl.CostEstimate(flops=8 * 2 * ROWS * D * H, bytes_accessed=30_000_000, transcendentals=0),
    )(
        fwd_acts[0], bwd_saved[0], bwd_cot[0], fwd_ids[0].T, bwd_ids[0].T, norm_gain, router[0].T,
        w_gate[0, 0], w_up[0, 0], w_down[0, 0],
    )
    fwd_out, bwd_grad = pl.pallas_call(
        leave,
        out_shape=(out, out),
        in_specs=[pl.BlockSpec(memory_space=pltpu.HBM)] * 2,
        out_specs=(pl.BlockSpec(memory_space=pltpu.HBM),) * 2,
        scratch_shapes=[vm(T, D), vm(T, D), pltpu.SemaphoreType.DMA((2, 4)), pltpu.SemaphoreType.DMA((2, 4))],
        name="leave",
        cost_estimate=pl.CostEstimate(flops=0, bytes_accessed=4 * 2 * T * D, transcendentals=0),
    )(fwd_out, bwd_grad)
    return fwd_out[None], bwd_grad[None]


def solution(mesh):
    rows = P("section", "expert", None)
    return jax.shard_map(
        per_device,
        mesh=mesh,
        in_specs=(
            rows, rows, rows, rows, rows, P("section", None), P("section", None, None),
            P("section", "expert", None, None), P("section", "expert", None, None), P("section", "expert", None, None),
        ),
        out_specs=(rows, rows),
        check_vma=False,
    )
```

```python
import functools

import jax
import jax.numpy as jnp
from jax import lax
from jax.experimental import pallas as pl
from jax.experimental.pallas import tpu as pltpu
from jax.sharding import PartitionSpec as P

MESH = pl.DeviceIdType.MESH
F32, BF16 = jnp.float32, jnp.bfloat16
route_scale = 2.5
epsilon = 1e-06

D, H, T, E = 3584, 1024, 128, 16
MAIN, OVER, PARTS = 16, 4, 4
WIDE = D // PARTS
BLOCK = MAIN * PARTS + OVER * PARTS
ROWS = E * (MAIN + OVER)
HALF = E // 2
HTILE = 256
NONE = -1000.0
XS = 4
QUARTER = T // XS
TURNS = (1, 3, 2, 0)
SPANS = {5: (0, 3 * MAIN), 6: (3 * MAIN, 2 * MAIN)}


def nt(a, b):
    return lax.dot_general(a, b, (((1,), (1,)), ((), ())), preferred_element_type=F32)


def nn(a, b):
    return jnp.dot(a, b, preferred_element_type=F32)


def iota(shape, axis):
    return lax.broadcasted_iota(jnp.int32, shape, axis)


def route(ids):
    at = iota((E, T), 0)
    hot = [(at == ids[k : k + 1, :]).astype(F32) for k in (0, 1)]
    tri = (iota((T, T), 0) < iota((T, T), 1)).astype(BF16)
    before = nn((hot[0] + hot[1]).astype(BF16), tri)
    line = iota((8, T), 0)
    rows = jnp.zeros((8, T), F32)
    for k in (0, 1):
        slot = jnp.sum(hot[k] * before, axis=0, keepdims=True)
        named = ids[k : k + 1, :].astype(F32)
        base = named * float(MAIN)
        rows = jnp.where(line == k, jnp.where(slot < MAIN, base + slot, NONE), rows)
        rows = jnp.where(line == 2 + k, jnp.where(slot < MAIN, NONE, base + slot - MAIN), rows)
        rows = jnp.where(line == 4 + k, named, rows)
    return rows


def stand(rows):
    return jnp.transpose(jnp.concatenate([rows, jnp.zeros((T - 8, T), F32)], axis=0))


def picks(rows, places, base, shift):
    at = (iota((T, T), 0) + base).astype(F32)
    return sum((at == rows[p : p + 1, :] + shift).astype(F32) for p in places).astype(BF16)


def gates(logits, columns):
    lanes = iota((T, E), 1).astype(F32)
    score = [
        jax.nn.sigmoid(jnp.sum(jnp.where(lanes == columns[:, 4 + k : 5 + k], logits, 0.0), axis=1, keepdims=True))
        for k in (0, 1)
    ]
    total = score[0] + score[1]
    return score, total, [route_scale * s / total for s in score]


def spread(places, values, shift):
    at = iota((T, E * MAIN), 1).astype(F32)
    return sum(jnp.where(at == p + shift, v, 0.0) for p, v in zip(places, values)).astype(BF16)


def kernel(
    fwd_hbm, saved_hbm, cot_hbm, idf_hbm, idb_hbm, gain_hbm, router_hbm, wg_hbm, wu_hbm, wd_hbm,
    of_hbm, ob_hbm,
    wg, wu, wd, a1s, a1r, a2s, a2r, a3s, a3r, r1r, r2r, ps, pr,
    xr, saved, normed, arr_f, arr_b, dg, du, gates_b, ups_b, scaled, router, gain,
    idf, idb, rowf, rowb, colf, colb, gf, gb,
    via, ssem, rsem, hsend, hrecv, vsend, vrecv, lsem, osem,
):
    s, e = lax.axis_index("section"), lax.axis_index("expert")
    layers = lax.axis_size("section")
    after, ahead = (s + 1) % layers, (s + layers - 1) % layers
    yhi, zed, core = e // HALF, e // 2 % 4, e % 2
    near, far = yhi * HALF, (1 - yhi) * HALF

    loads = [
        pltpu.make_async_copy(src, dst, lsem.at[i])
        for i, (src, dst) in enumerate(
            [(saved_hbm, saved), (idb_hbm, idb), (gain_hbm, gain), (idf_hbm, idf),
             (router_hbm, router), (wg_hbm, wg), (wu_hbm, wu), (wd_hbm, wd)]
        )
    ]
    for load in loads[:4]:
        load.start()

    barrier = pltpu.get_barrier_semaphore()

    def greet(d, _):
        pl.semaphore_signal(barrier, inc=1, device_id=(s, (e + d) % E), device_id_type=MESH)
        return 0

    def greet_section(d, _):
        pl.semaphore_signal(barrier, inc=1, device_id=((s + d) % layers, e), device_id_type=MESH)
        return 0

    lax.fori_loop(1, layers, greet_section, 0)
    lax.fori_loop(1, E, greet, 0)

    across, band = s % XS, s // XS
    blocks = ((fwd_hbm, arr_f), (cot_hbm, arr_b))
    ways = ((0, 3, 2, 1), (3, 0, 1, 2))
    towards = (after, ahead)
    at_end = (across == XS - 1, across == 0)

    def quarter(n, j):
        rows = pl.ds(j * QUARTER, QUARTER)
        return pltpu.make_async_remote_copy(
            blocks[n][0].at[rows], blocks[n][1].at[rows], hsend.at[n, j], hrecv.at[n, j],
            device_id=(towards[n], e), device_id_type=MESH)

    def detour(n, j):
        return pltpu.make_async_remote_copy(
            blocks[n][0].at[pl.ds(j * QUARTER, QUARTER)], via.at[n], hsend.at[n, j], vrecv.at[n],
            device_id=((1 - band) * XS + ways[n][j], e), device_id_type=MESH)

    def onward(n, j):
        return pltpu.make_async_remote_copy(
            via.at[n], blocks[n][1].at[pl.ds(j * QUARTER, QUARTER)], vsend.at[n], hrecv.at[n, j],
            device_id=(band * XS + ways[n][0], e), device_id_type=MESH)

    def hop(n):
        for j in range(1, XS):

            @pl.when(at_end[n])
            def _():
                detour(n, j).start()

            @pl.when(jnp.logical_not(at_end[n]))
            def _():
                quarter(n, j).start()

        quarter(n, 0).start()

    def relay(n):
        for j in range(1, XS):

            @pl.when(across == ways[n][j])
            def _():
                detour(n, j).wait_recv()
                onward(n, j).start()

    def hop_arrive(n):
        for j in range(XS):
            quarter(n, j).wait_recv()

    def hop_sent(n):
        for j in range(XS):
            quarter(n, j).wait_send()
        for j in range(1, XS):

            @pl.when(across == ways[n][j])
            def _():
                onward(n, j).wait_send()

    def peer(half, dz, dc):
        return half + (zed + dz) % 4 * 2 + (core + dc) % 2

    def remote(k, src, dst, p, at):
        first, count = SPANS.get(k, (0, src.shape[1]))
        span = pl.ds(first, count)
        return pltpu.make_async_remote_copy(
            src.at[p, span], dst.at[at, span], ssem.at[k, p], rsem.at[k, at], device_id=(s, p), device_id_type=MESH)

    def own(k, src, dst):
        first, count = SPANS.get(k, (0, src.shape[1]))
        span = pl.ds(first, count)
        return pltpu.make_async_copy(src.at[e, span], dst.at[e, span], rsem.at[k, e])

    def others(act):
        def step(d, _):
            act((e + d) % E)
            return 0

        lax.fori_loop(1, E, step, 0)

    def send_far(k, src, dst):
        for dc in (0, 1):
            for dz in TURNS:
                remote(k, src, dst, peer(far, dz, dc), e).start()

    def send_near(k, src, dst):
        for dc in (1, 0):
            for dz in TURNS:
                if (dz, dc) != (0, 0):
                    remote(k, src, dst, peer(near, dz, dc), e).start()
        own(k, src, dst).start()

    def send(k, src, dst):
        send_far(k, src, dst)
        send_near(k, src, dst)

    def arrive(k, src, dst):
        others(lambda p: remote(k, src, dst, p, p).wait_recv())
        own(k, src, dst).wait()

    def sent(k, src, dst):
        others(lambda p: remote(k, src, dst, p, e).wait_send())

    def norm(x_ref, by, out):
        x = x_ref[...].astype(F32)
        inv = lax.rsqrt(jnp.sum(x * x, axis=1, keepdims=True) * (1.0 / D) + epsilon)
        out[...] = (x * inv * by[...].astype(F32)).astype(BF16)
        return inv

    def pack(x_ref, rows, buf, first):
        base = first * MAIN
        main = picks(rows, (0, 1), base, 0.0)

        def step(q, _):
            got = nn(main, x_ref[:, pl.ds(pl.multiple_of(q * WIDE, 128), WIDE)]).astype(BF16)
            buf[pl.ds(first, HALF), pl.ds(pl.multiple_of(q * MAIN + MAIN, MAIN), MAIN), :] = got.reshape(HALF, MAIN, WIDE)
            return 0

        lax.fori_loop(0, PARTS, step, 0)
        over = sum(
            nn(picks(rows, (2, 3), base, float(OVER * q)), x_ref[:, q * WIDE : (q + 1) * WIDE])
            for q in range(PARTS)
        )
        buf[pl.ds(first, HALF), 0:MAIN, :] = over.astype(BF16).reshape(HALF, MAIN, WIDE)

    def dispatch(k, x_ref, rows, src, dst):
        pack(x_ref, rows, src, far)
        send_far(k, src, dst)
        pack(x_ref, rows, src, near)
        send_near(k, src, dst)

    def unpack(buf, out):
        tail = buf[:, 0:MAIN, :].reshape(E * MAIN, WIDE)
        row, lane = iota((E * OVER, E * MAIN), 0), iota((E * OVER, E * MAIN), 1)

        def step(q, _):
            columns = pl.ds(pl.multiple_of(q * WIDE, 128), WIDE)
            out[0 : E * MAIN, columns] = buf[:, pl.ds(pl.multiple_of(q * MAIN + MAIN, MAIN), MAIN), :].reshape(E * MAIN, WIDE)
            pick = (lane == (row // OVER) * MAIN + OVER * q + row % OVER).astype(BF16)
            out[E * MAIN : ROWS, columns] = nn(pick, tail).astype(BF16)
            return 0

        lax.fori_loop(0, PARTS, step, 0)

    def lay(q, buf, value):
        low = value.astype(BF16)
        buf[:, pl.ds(pl.multiple_of(q * MAIN + MAIN, MAIN), MAIN), :] = low[0 : E * MAIN].reshape(E, MAIN, WIDE)
        row, lane = iota((E * MAIN, E * OVER), 0), iota((E * MAIN, E * OVER), 1)
        here = (lane == (row // MAIN) * OVER + row % OVER) & (row % MAIN // OVER == q)
        return nn(here.astype(BF16), low[E * MAIN : ROWS])

    scope = jax.named_scope
    with scope("start"):
        loads[1].wait()
        rowb[...] = route(idb[...])
        loads[0].wait()
        loads[2].wait()
        gb[:, 0:1] = norm(saved, gain, normed)
        pack(normed, rowb, a1s, far)
    with scope("barrier"):
        pl.semaphore_wait(barrier, E - 1 + layers - 1)
    with scope("rows_b_out"):
        hop(1)
        hop(0)
        send_far(0, a1s, a1r)
        pack(normed, rowb, a1s, near)
        send_near(0, a1s, a1r)
        for load in loads[4:]:
            load.start()
    with scope("gating_b"):
        colb[...] = stand(rowb[...])
        loads[4].wait()
        score, total, weight = gates(nt(normed[...], router[...]), colb)
        gb[:, 1:2], gb[:, 2:3], gb[:, 3:4] = score[0], score[1], total
        gb[:, 4:5], gb[:, 5:6] = weight[0], weight[1]
        loads[3].wait()
        rowf[...] = route(idf[...])
    with scope("relay"):
        relay(1)
        relay(0)
    with scope("wait_hop_b"):
        hop_arrive(1)
    with scope("cot_near_out"):
        dispatch(1, arr_b, rowb, a2s, a2r)
    with scope("wait_hop_f"):
        hop_arrive(0)
    with scope("fwd_near_pack"):
        norm(arr_f, gain, normed)
        dispatch(2, normed, rowf, a3s, a3r)
        colf[...] = stand(rowf[...])
        score, total, weight = gates(nt(normed[...], router[...]), colf)
        gf[:, 0:1], gf[:, 1:2] = weight[0], weight[1]
    with scope("wait_rows_b"):
        for load in loads[5:]:
            load.wait()
        arrive(0, a1s, a1r)
    with scope("gate_up_b"):
        unpack(a1r, xr)

        def gate_up(n, _):
            columns = pl.ds(pl.multiple_of(n * HTILE, HTILE), HTILE)
            gates_b[:, columns] = nn(xr[...], wg[:, columns])
            ups_b[:, columns] = nn(xr[...], wu[:, columns])
            return 0

        lax.fori_loop(0, H // HTILE, gate_up, 0)
    with scope("wait_cot"):
        arrive(1, a2s, a2r)

    def hidden(n, prod):
        columns = pl.ds(pl.multiple_of(n * HTILE, HTILE), HTILE)
        gate, up = gates_b[:, columns], ups_b[:, columns]
        grad = nt(xr[...], wd[columns, :])
        sig = jax.nn.sigmoid(gate)
        act = (gate * sig * up).astype(BF16).astype(F32)
        dg[:, columns] = (grad * up * sig * (1.0 + gate * (1.0 - sig))).astype(BF16)
        du[:, columns] = (grad * gate * sig).astype(BF16)
        return prod + jnp.sum(act * grad, axis=1, keepdims=True)

    with scope("hidden_b"):
        unpack(a2r, xr)
        prod = lax.fori_loop(0, H // HTILE, hidden, jnp.zeros((ROWS, 1), F32))
    prod = jnp.broadcast_to(prod, (ROWS, T)).astype(BF16)
    row, lane = iota((E * MAIN, E * OVER), 0), iota((E * MAIN, E * OVER), 1)
    here = (lane == (row // MAIN) * OVER + row % OVER).astype(BF16)
    over = nn(here, prod[E * MAIN : ROWS]).astype(BF16)
    side = iota((E * MAIN, T), 1) < T // 2
    ps[...] = jnp.where(side, prod[0 : E * MAIN].astype(F32), over.astype(F32)).astype(BF16).reshape(E, MAIN, T)
    send(3, ps, pr)
    with scope("wait_rows_b_sent"):
        sent(0, a1s, a1r)

    def unit(q, over):
        rows = pl.ds(pl.multiple_of(q * WIDE, 128), WIDE)
        return over + lay(q, a1s, nt(dg[...], wg[rows, :]) + nt(du[...], wu[rows, :]))

    with scope("unit_b"):
        over = lax.fori_loop(0, PARTS, unit, jnp.zeros((E * MAIN, WIDE), F32))
    a1s[:, 0:MAIN, :] = over.astype(BF16).reshape(E, MAIN, WIDE)
    send(4, a1s, r1r)

    with scope("wait_rows_f"):
        arrive(2, a3s, a3r)

    def hidden_f(n, _):
        columns = pl.ds(pl.multiple_of(n * HTILE, HTILE), HTILE)
        gate, up = nn(xr[...], wg[:, columns]), nn(xr[...], wu[:, columns])
        dg[:, columns] = (gate * jax.nn.sigmoid(gate) * up).astype(BF16)
        return 0

    with scope("hidden_f"):
        unpack(a3r, xr)
        lax.fori_loop(0, H // HTILE, hidden_f, 0)
    with scope("wait_cot_sent"):
        sent(1, a2s, a2r)

    def down(q, over):
        columns = pl.ds(pl.multiple_of(q * WIDE, 128), WIDE)
        return over + lay(q, a2s, nn(dg[...], wd[:, columns]))

    with scope("down_f"):
        over = lax.fori_loop(0, PARTS, down, jnp.zeros((E * MAIN, WIDE), F32))
    a2s[:, 0:MAIN, :] = over.astype(BF16).reshape(E, MAIN, WIDE)
    send(5, a2s, r2r)
    send(6, a2s, r2r)

    with scope("wait_unit"):
        arrive(3, ps, pr)
        arrive(4, a1s, r1r)
    places = [colb[:, p : p + 1] for p in range(4)]
    score, total = [gb[:, 1:2], gb[:, 2:3]], gb[:, 3:4]
    weight = [gb[:, 4:5], gb[:, 5:6]]
    inv = gb[:, 0:1]
    one = jnp.ones((T, 1), F32)
    product = []
    for k in (0, 1):
        main = nn(spread([places[k]], [one], 0.0), pr[...].reshape(E * MAIN, T))[:, 0:1]
        over = nn(spread([places[2 + k]], [one], 0.0), pr[...].reshape(E * MAIN, T))[:, T // 2 : T // 2 + 1]
        product.append(main + over)
    mixed = (product[0] * weight[0] + product[1] * weight[1]) * (1.0 / route_scale)
    lanes = iota((T, E), 1).astype(F32)
    dlogits = jnp.zeros((T, E), F32)
    for k in (0, 1):
        dlogit = route_scale / total * (product[k] - mixed) * score[k] * (1.0 - score[k])
        dlogits += jnp.where(lanes == colb[:, 4 + k : 5 + k], dlogit, 0.0)
    dlogits = dlogits.astype(BF16)
    main_w = spread(places[0:2], weight, 0.0)

    def grad_in(q, dot):
        columns = pl.ds(pl.multiple_of(q * WIDE, 128), WIDE)
        over_w = spread(places[2:4], weight, (OVER * q).astype(F32))
        got = nn(main_w, r1r[:, pl.ds(pl.multiple_of(q * MAIN + MAIN, MAIN), MAIN), :].reshape(E * MAIN, WIDE))
        got += nn(over_w, r1r[:, 0:MAIN, :].reshape(E * MAIN, WIDE))
        got += nn(dlogits, router[:, columns])
        got *= gain[:, columns].astype(F32)
        scaled[:, columns] = got
        return dot + jnp.sum(got * saved[:, columns].astype(F32), axis=1, keepdims=True)

    with scope("finish_b"):
        dot = lax.fori_loop(0, PARTS, grad_in, jnp.zeros((T, 1), F32)) * (1.0 / D)
    back = inv * inv * inv * dot

    def finish_b(q, _):
        columns = pl.ds(pl.multiple_of(q * WIDE, 128), WIDE)
        dx = inv * scaled[:, columns] - saved[:, columns].astype(F32) * back
        saved[:, columns] = (arr_b[:, columns].astype(F32) + dx).astype(BF16)
        return 0

    with scope("finish_b2"):
        lax.fori_loop(0, PARTS, finish_b, 0)
    out_b = pltpu.make_async_copy(saved, ob_hbm, osem.at[0])
    out_b.start()
    pieces = [pl.ds(i * (D // 2), D // 2) for i in (0, 1)]
    out_f = [pltpu.make_async_copy(normed.at[:, piece], of_hbm.at[:, piece], osem.at[1 + i]) for i, piece in enumerate(pieces)]

    places_f = [colf[:, p : p + 1] for p in range(4)]
    weight_f = [gf[:, 0:1], gf[:, 1:2]]
    main_f = spread(places_f[0:2], weight_f, 0.0)
    def finish_f(q, _):
        columns = pl.ds(pl.multiple_of(q * WIDE, 128), WIDE)
        over_w = spread(places_f[2:4], weight_f, (OVER * q).astype(F32))
        got = nn(main_f, r2r[:, pl.ds(pl.multiple_of(q * MAIN + MAIN, MAIN), MAIN), :].reshape(E * MAIN, WIDE))
        got += nn(over_w, r2r[:, 0:MAIN, :].reshape(E * MAIN, WIDE))
        normed[:, columns] = (arr_f[:, columns].astype(F32) + got).astype(BF16)
        return 0

    with scope("finish_f"):
        arrive(5, a2s, r2r)
        lax.fori_loop(0, PARTS // 2, finish_f, 0)
        out_f[0].start()
        arrive(6, a2s, r2r)
        lax.fori_loop(PARTS // 2, PARTS, finish_f, 0)
        out_f[1].start()
    with scope("drain"):
        hop_sent(0)
        hop_sent(1)
        sent(2, a3s, a3r)
        sent(3, ps, pr)
        sent(4, a1s, r1r)
        sent(5, a2s, r2r)
        sent(6, a2s, r2r)
        out_b.wait()
        out_f[0].wait()
        out_f[1].wait()


def leave(f_hbm, b_hbm, of_hbm, ob_hbm, f_ref, b_ref, in_sem, out_sem):
    pairs = []
    for i, (src, mid, dst) in enumerate(((f_hbm, f_ref, of_hbm), (b_hbm, b_ref, ob_hbm))):
        for j in range(4):
            part = pl.ds(j * (T // 4), T // 4)
            pairs.append(
                (pltpu.make_async_copy(src.at[part], mid.at[part], in_sem.at[i, j]),
                 pltpu.make_async_copy(mid.at[part], dst.at[part], out_sem.at[i, j]))
            )
    for come, _ in pairs:
        come.start()
    for come, go in pairs:
        come.wait()
        go.start()
    for _, go in pairs:
        go.wait()


def per_device(fwd_acts, bwd_saved, bwd_cot, fwd_ids, bwd_ids, norm_gain, router, w_gate, w_up, w_down):
    def vm(*shape, dtype=BF16):
        return pltpu.VMEM(shape, dtype)

    block = (E, BLOCK, WIDE)
    scratch = [
        vm(D, H), vm(D, H), vm(H, D),
        *[vm(*block) for _ in range(8)],
        vm(E, MAIN, T), vm(E, MAIN, T),
        vm(ROWS, D),
        *[vm(T, D) for _ in range(4)],
        vm(ROWS, H), vm(ROWS, H), vm(ROWS, H, dtype=F32), vm(ROWS, H, dtype=F32),
        vm(T, D, dtype=F32),
        vm(E, D), vm(1, D),
        vm(2, T, dtype=jnp.int32), vm(2, T, dtype=jnp.int32),
        *[vm(8, T, dtype=F32) for _ in range(2)],
        *[vm(T, T, dtype=F32) for _ in range(4)],
        vm(2, QUARTER, D),
        pltpu.SemaphoreType.DMA((7, E)), pltpu.SemaphoreType.DMA((7, E)),
        pltpu.SemaphoreType.DMA((2, XS)), pltpu.SemaphoreType.DMA((2, XS)),
        pltpu.SemaphoreType.DMA((2,)), pltpu.SemaphoreType.DMA((2,)),
        pltpu.SemaphoreType.DMA((8,)), pltpu.SemaphoreType.DMA((3,)),
    ]
    out = jax.ShapeDtypeStruct((T, D), BF16)
    fwd_out, bwd_grad = pl.pallas_call(
        kernel,
        out_shape=(out, out),
        in_specs=[pl.BlockSpec(memory_space=pltpu.HBM)] * 10,
        out_specs=(pl.BlockSpec(memory_space=pltpu.HBM),) * 2,
        scratch_shapes=scratch,
        name="layer",
        compiler_params=pltpu.CompilerParams(
            collective_id=0, has_side_effects=True, vmem_limit_bytes=62 * 1024 * 1024
        ),
        cost_estimate=pl.CostEstimate(flops=8 * 2 * ROWS * D * H, bytes_accessed=30_000_000, transcendentals=0),
    )(
        fwd_acts[0], bwd_saved[0], bwd_cot[0], fwd_ids[0].T, bwd_ids[0].T, norm_gain, router[0].T,
        w_gate[0, 0], w_up[0, 0], w_down[0, 0],
    )
    fwd_out, bwd_grad = pl.pallas_call(
        leave,
        out_shape=(out, out),
        in_specs=[pl.BlockSpec(memory_space=pltpu.HBM)] * 2,
        out_specs=(pl.BlockSpec(memory_space=pltpu.HBM),) * 2,
        scratch_shapes=[vm(T, D), vm(T, D), pltpu.SemaphoreType.DMA((2, 4)), pltpu.SemaphoreType.DMA((2, 4))],
        name="leave",
        cost_estimate=pl.CostEstimate(flops=0, bytes_accessed=4 * 2 * T * D, transcendentals=0),
    )(fwd_out, bwd_grad)
    return fwd_out[None], bwd_grad[None]


def solution(mesh):
    rows = P("section", "expert", None)
    return jax.shard_map(
        per_device,
        mesh=mesh,
        in_specs=(
            rows, rows, rows, rows, rows, P("section", None), P("section", None, None),
            P("section", "expert", None, None), P("section", "expert", None, None), P("section", "expert", None, None),
        ),
        out_specs=(rows, rows),
        check_vma=False,
    )
```

```python
import functools

import jax
import jax.numpy as jnp
from jax import lax
from jax.experimental import pallas as pl
from jax.experimental.pallas import tpu as pltpu
from jax.sharding import PartitionSpec as P

MESH = pl.DeviceIdType.MESH
F32, BF16 = jnp.float32, jnp.bfloat16
route_scale = 2.5
epsilon = 1e-06

D, H, T, E = 3584, 1024, 128, 16
MAIN, OVER, PARTS = 16, 4, 4
WIDE = D // PARTS
BLOCK = MAIN * PARTS + OVER * PARTS
ROWS = E * (MAIN + OVER)
HALF = E // 2
HTILE = 256
NONE = -1000.0
XS = 4
QUARTER = T // XS
TURNS = (1, 3, 2, 0)
SPANS = {5: (0, 3 * MAIN), 6: (3 * MAIN, 2 * MAIN)}


def nt(a, b):
    return lax.dot_general(a, b, (((1,), (1,)), ((), ())), preferred_element_type=F32)


def nn(a, b):
    return jnp.dot(a, b, preferred_element_type=F32)


def iota(shape, axis):
    return lax.broadcasted_iota(jnp.int32, shape, axis)


def route(ids):
    at = iota((E, T), 0)
    hot = [(at == ids[k : k + 1, :]).astype(F32) for k in (0, 1)]
    tri = (iota((T, T), 0) < iota((T, T), 1)).astype(BF16)
    before = nn((hot[0] + hot[1]).astype(BF16), tri)
    line = iota((8, T), 0)
    rows = jnp.zeros((8, T), F32)
    for k in (0, 1):
        slot = jnp.sum(hot[k] * before, axis=0, keepdims=True)
        named = ids[k : k + 1, :].astype(F32)
        base = named * float(MAIN)
        rows = jnp.where(line == k, jnp.where(slot < MAIN, base + slot, NONE), rows)
        rows = jnp.where(line == 2 + k, jnp.where(slot < MAIN, NONE, base + slot - MAIN), rows)
        rows = jnp.where(line == 4 + k, named, rows)
    return rows


def stand(rows):
    return jnp.transpose(jnp.concatenate([rows, jnp.zeros((T - 8, T), F32)], axis=0))


def picks(rows, places, base, shift):
    at = (iota((T, T), 0) + base).astype(F32)
    return sum((at == rows[p : p + 1, :] + shift).astype(F32) for p in places).astype(BF16)


def gates(logits, columns):
    lanes = iota((T, E), 1).astype(F32)
    score = [
        jax.nn.sigmoid(jnp.sum(jnp.where(lanes == columns[:, 4 + k : 5 + k], logits, 0.0), axis=1, keepdims=True))
        for k in (0, 1)
    ]
    total = score[0] + score[1]
    return score, total, [route_scale * s / total for s in score]


def spread(places, values, shift):
    at = iota((T, E * MAIN), 1).astype(F32)
    return sum(jnp.where(at == p + shift, v, 0.0) for p, v in zip(places, values)).astype(BF16)


def kernel(
    fwd_hbm, saved_hbm, cot_hbm, idf_hbm, idb_hbm, gain_hbm, router_hbm, wg_hbm, wu_hbm, wd_hbm,
    of_hbm, ob_hbm,
    wg, wu, wd, a1s, a1r, a2s, a2r, a3s, a3r, r1r, r2r, ps, pr,
    xr, saved, normed, arr_f, arr_b, dg, du, gates_b, ups_b, scaled, router, gain,
    idf, idb, rowf, rowb, colf, colb, gf, gb,
    via, ssem, rsem, hsend, hrecv, vsend, vrecv, lsem, osem,
):
    s, e = lax.axis_index("section"), lax.axis_index("expert")
    layers = lax.axis_size("section")
    after, ahead = (s + 1) % layers, (s + layers - 1) % layers
    yhi, zed, core = e // HALF, e // 2 % 4, e % 2
    near, far = yhi * HALF, (1 - yhi) * HALF

    loads = [
        pltpu.make_async_copy(src, dst, lsem.at[i])
        for i, (src, dst) in enumerate(
            [(saved_hbm, saved), (idb_hbm, idb), (gain_hbm, gain), (idf_hbm, idf),
             (router_hbm, router), (wg_hbm, wg), (wu_hbm, wu), (wd_hbm, wd)]
        )
    ]
    for load in loads[:4]:
        load.start()

    barrier = pltpu.get_barrier_semaphore()

    def greet(d, _):
        pl.semaphore_signal(barrier, inc=1, device_id=(s, (e + d) % E), device_id_type=MESH)
        return 0

    def greet_section(d, _):
        pl.semaphore_signal(barrier, inc=1, device_id=((s + d) % layers, e), device_id_type=MESH)
        return 0

    lax.fori_loop(1, layers, greet_section, 0)
    lax.fori_loop(1, E, greet, 0)

    across, band = s % XS, s // XS
    blocks = ((fwd_hbm, arr_f), (cot_hbm, arr_b))
    ways = ((0, 3, 2, 1), (3, 0, 1, 2))
    towards = (after, ahead)
    at_end = (across == XS - 1, across == 0)

    def quarter(n, j):
        rows = pl.ds(j * QUARTER, QUARTER)
        return pltpu.make_async_remote_copy(
            blocks[n][0].at[rows], blocks[n][1].at[rows], hsend.at[n, j], hrecv.at[n, j],
            device_id=(towards[n], e), device_id_type=MESH)

    def detour(n, j):
        return pltpu.make_async_remote_copy(
            blocks[n][0].at[pl.ds(j * QUARTER, QUARTER)], via.at[n], hsend.at[n, j], vrecv.at[n],
            device_id=((1 - band) * XS + ways[n][j], e), device_id_type=MESH)

    def onward(n, j):
        return pltpu.make_async_remote_copy(
            via.at[n], blocks[n][1].at[pl.ds(j * QUARTER, QUARTER)], vsend.at[n], hrecv.at[n, j],
            device_id=(band * XS + ways[n][0], e), device_id_type=MESH)

    def hop(n):
        for j in range(1, XS):

            @pl.when(at_end[n])
            def _():
                detour(n, j).start()

            @pl.when(jnp.logical_not(at_end[n]))
            def _():
                quarter(n, j).start()

        quarter(n, 0).start()

    def relay(n):
        for j in range(1, XS):

            @pl.when(across == ways[n][j])
            def _():
                detour(n, j).wait_recv()
                onward(n, j).start()

    def hop_arrive(n):
        for j in range(XS):
            quarter(n, j).wait_recv()

    def hop_sent(n):
        for j in range(XS):
            quarter(n, j).wait_send()
        for j in range(1, XS):

            @pl.when(across == ways[n][j])
            def _():
                onward(n, j).wait_send()

    def peer(half, dz, dc):
        return half + (zed + dz) % 4 * 2 + (core + dc) % 2

    def remote(k, src, dst, p, at):
        first, count = SPANS.get(k, (0, src.shape[1]))
        span = pl.ds(first, count)
        return pltpu.make_async_remote_copy(
            src.at[p, span], dst.at[at, span], ssem.at[k, p], rsem.at[k, at], device_id=(s, p), device_id_type=MESH)

    def own(k, src, dst):
        first, count = SPANS.get(k, (0, src.shape[1]))
        span = pl.ds(first, count)
        return pltpu.make_async_copy(src.at[e, span], dst.at[e, span], rsem.at[k, e])

    def others(act):
        def step(d, _):
            act((e + d) % E)
            return 0

        lax.fori_loop(1, E, step, 0)

    def send_far(k, src, dst):
        for dc in (0, 1):
            for dz in TURNS:
                remote(k, src, dst, peer(far, dz, dc), e).start()

    def send_near(k, src, dst):
        for dc in (1, 0):
            for dz in TURNS:
                if (dz, dc) != (0, 0):
                    remote(k, src, dst, peer(near, dz, dc), e).start()
        own(k, src, dst).start()

    def send(k, src, dst):
        send_far(k, src, dst)
        send_near(k, src, dst)

    def arrive(k, src, dst):
        others(lambda p: remote(k, src, dst, p, p).wait_recv())
        own(k, src, dst).wait()

    def sent(k, src, dst):
        others(lambda p: remote(k, src, dst, p, e).wait_send())

    def norm(x_ref, by, out):
        x = x_ref[...].astype(F32)
        inv = lax.rsqrt(jnp.sum(x * x, axis=1, keepdims=True) * (1.0 / D) + epsilon)
        out[...] = (x * inv * by[...].astype(F32)).astype(BF16)
        return inv

    def pack(x_ref, rows, buf, first):
        base = first * MAIN
        main = picks(rows, (0, 1), base, 0.0)

        def step(q, _):
            got = nn(main, x_ref[:, pl.ds(pl.multiple_of(q * WIDE, 128), WIDE)]).astype(BF16)
            buf[pl.ds(first, HALF), pl.ds(pl.multiple_of(q * MAIN + MAIN, MAIN), MAIN), :] = got.reshape(HALF, MAIN, WIDE)
            return 0

        lax.fori_loop(0, PARTS, step, 0)
        over = sum(
            nn(picks(rows, (2, 3), base, float(OVER * q)), x_ref[:, q * WIDE : (q + 1) * WIDE])
            for q in range(PARTS)
        )
        buf[pl.ds(first, HALF), 0:MAIN, :] = over.astype(BF16).reshape(HALF, MAIN, WIDE)

    def dispatch(k, x_ref, rows, src, dst):
        pack(x_ref, rows, src, far)
        send_far(k, src, dst)
        pack(x_ref, rows, src, near)
        send_near(k, src, dst)

    def unpack(buf, out):
        tail = buf[:, 0:MAIN, :].reshape(E * MAIN, WIDE)
        row, lane = iota((E * OVER, E * MAIN), 0), iota((E * OVER, E * MAIN), 1)

        def step(q, _):
            columns = pl.ds(pl.multiple_of(q * WIDE, 128), WIDE)
            out[0 : E * MAIN, columns] = buf[:, pl.ds(pl.multiple_of(q * MAIN + MAIN, MAIN), MAIN), :].reshape(E * MAIN, WIDE)
            pick = (lane == (row // OVER) * MAIN + OVER * q + row % OVER).astype(BF16)
            out[E * MAIN : ROWS, columns] = nn(pick, tail).astype(BF16)
            return 0

        lax.fori_loop(0, PARTS, step, 0)

    def lay(q, buf, value):
        low = value.astype(BF16)
        buf[:, pl.ds(pl.multiple_of(q * MAIN + MAIN, MAIN), MAIN), :] = low[0 : E * MAIN].reshape(E, MAIN, WIDE)
        row, lane = iota((E * MAIN, E * OVER), 0), iota((E * MAIN, E * OVER), 1)
        here = (lane == (row // MAIN) * OVER + row % OVER) & (row % MAIN // OVER == q)
        return nn(here.astype(BF16), low[E * MAIN : ROWS])

    scope = jax.named_scope
    with scope("start"):
        loads[1].wait()
        rowb[...] = route(idb[...])
        loads[0].wait()
        loads[2].wait()
        gb[:, 0:1] = norm(saved, gain, normed)
        pack(normed, rowb, a1s, far)
    with scope("barrier"):
        pl.semaphore_wait(barrier, E - 1 + layers - 1)
    with scope("rows_b_out"):
        hop(1)
        hop(0)
        send_far(0, a1s, a1r)
        pack(normed, rowb, a1s, near)
        send_near(0, a1s, a1r)
        for load in loads[4:]:
            load.start()
    with scope("relay"):
        relay(1)
        relay(0)
    with scope("gating_b"):
        colb[...] = stand(rowb[...])
        loads[4].wait()
        score, total, weight = gates(nt(normed[...], router[...]), colb)
        gb[:, 1:2], gb[:, 2:3], gb[:, 3:4] = score[0], score[1], total
        gb[:, 4:5], gb[:, 5:6] = weight[0], weight[1]
        loads[3].wait()
        rowf[...] = route(idf[...])
    with scope("wait_hop_b"):
        hop_arrive(1)
    with scope("cot_near_out"):
        dispatch(1, arr_b, rowb, a2s, a2r)
    with scope("wait_hop_f"):
        hop_arrive(0)
    with scope("fwd_near_pack"):
        norm(arr_f, gain, normed)
        dispatch(2, normed, rowf, a3s, a3r)
        colf[...] = stand(rowf[...])
        score, total, weight = gates(nt(normed[...], router[...]), colf)
        gf[:, 0:1], gf[:, 1:2] = weight[0], weight[1]
    with scope("wait_rows_b"):
        for load in loads[5:]:
            load.wait()
        arrive(0, a1s, a1r)
    with scope("gate_up_b"):
        unpack(a1r, xr)

        def gate_up(n, _):
            columns = pl.ds(pl.multiple_of(n * HTILE, HTILE), HTILE)
            gates_b[:, columns] = nn(xr[...], wg[:, columns])
            ups_b[:, columns] = nn(xr[...], wu[:, columns])
            return 0

        lax.fori_loop(0, H // HTILE, gate_up, 0)
    with scope("wait_cot"):
        arrive(1, a2s, a2r)

    def hidden(n, prod):
        columns = pl.ds(pl.multiple_of(n * HTILE, HTILE), HTILE)
        gate, up = gates_b[:, columns], ups_b[:, columns]
        grad = nt(xr[...], wd[columns, :])
        sig = jax.nn.sigmoid(gate)
        act = (gate * sig * up).astype(BF16).astype(F32)
        dg[:, columns] = (grad * up * sig * (1.0 + gate * (1.0 - sig))).astype(BF16)
        du[:, columns] = (grad * gate * sig).astype(BF16)
        return prod + jnp.sum(act * grad, axis=1, keepdims=True)

    with scope("hidden_b"):
        unpack(a2r, xr)
        prod = lax.fori_loop(0, H // HTILE, hidden, jnp.zeros((ROWS, 1), F32))
    prod = jnp.broadcast_to(prod, (ROWS, T)).astype(BF16)
    row, lane = iota((E * MAIN, E * OVER), 0), iota((E * MAIN, E * OVER), 1)
    here = (lane == (row // MAIN) * OVER + row % OVER).astype(BF16)
    over = nn(here, prod[E * MAIN : ROWS]).astype(BF16)
    side = iota((E * MAIN, T), 1) < T // 2
    ps[...] = jnp.where(side, prod[0 : E * MAIN].astype(F32), over.astype(F32)).astype(BF16).reshape(E, MAIN, T)
    send(3, ps, pr)
    with scope("wait_rows_b_sent"):
        sent(0, a1s, a1r)

    def unit(q, over):
        rows = pl.ds(pl.multiple_of(q * WIDE, 128), WIDE)
        return over + lay(q, a1s, nt(dg[...], wg[rows, :]) + nt(du[...], wu[rows, :]))

    with scope("unit_b"):
        over = lax.fori_loop(0, PARTS, unit, jnp.zeros((E * MAIN, WIDE), F32))
    a1s[:, 0:MAIN, :] = over.astype(BF16).reshape(E, MAIN, WIDE)
    send(4, a1s, r1r)

    with scope("wait_rows_f"):
        arrive(2, a3s, a3r)

    def hidden_f(n, _):
        columns = pl.ds(pl.multiple_of(n * HTILE, HTILE), HTILE)
        gate, up = nn(xr[...], wg[:, columns]), nn(xr[...], wu[:, columns])
        dg[:, columns] = (gate * jax.nn.sigmoid(gate) * up).astype(BF16)
        return 0

    with scope("hidden_f"):
        unpack(a3r, xr)
        lax.fori_loop(0, H // HTILE, hidden_f, 0)
    with scope("wait_cot_sent"):
        sent(1, a2s, a2r)

    def down(q, over):
        columns = pl.ds(pl.multiple_of(q * WIDE, 128), WIDE)
        return over + lay(q, a2s, nn(dg[...], wd[:, columns]))

    with scope("down_f"):
        over = lax.fori_loop(0, PARTS, down, jnp.zeros((E * MAIN, WIDE), F32))
    a2s[:, 0:MAIN, :] = over.astype(BF16).reshape(E, MAIN, WIDE)
    send(5, a2s, r2r)
    send(6, a2s, r2r)

    with scope("wait_unit"):
        arrive(3, ps, pr)
        arrive(4, a1s, r1r)
    places = [colb[:, p : p + 1] for p in range(4)]
    score, total = [gb[:, 1:2], gb[:, 2:3]], gb[:, 3:4]
    weight = [gb[:, 4:5], gb[:, 5:6]]
    inv = gb[:, 0:1]
    one = jnp.ones((T, 1), F32)
    product = []
    for k in (0, 1):
        main = nn(spread([places[k]], [one], 0.0), pr[...].reshape(E * MAIN, T))[:, 0:1]
        over = nn(spread([places[2 + k]], [one], 0.0), pr[...].reshape(E * MAIN, T))[:, T // 2 : T // 2 + 1]
        product.append(main + over)
    mixed = (product[0] * weight[0] + product[1] * weight[1]) * (1.0 / route_scale)
    lanes = iota((T, E), 1).astype(F32)
    dlogits = jnp.zeros((T, E), F32)
    for k in (0, 1):
        dlogit = route_scale / total * (product[k] - mixed) * score[k] * (1.0 - score[k])
        dlogits += jnp.where(lanes == colb[:, 4 + k : 5 + k], dlogit, 0.0)
    dlogits = dlogits.astype(BF16)
    main_w = spread(places[0:2], weight, 0.0)

    def grad_in(q, dot):
        columns = pl.ds(pl.multiple_of(q * WIDE, 128), WIDE)
        over_w = spread(places[2:4], weight, (OVER * q).astype(F32))
        got = nn(main_w, r1r[:, pl.ds(pl.multiple_of(q * MAIN + MAIN, MAIN), MAIN), :].reshape(E * MAIN, WIDE))
        got += nn(over_w, r1r[:, 0:MAIN, :].reshape(E * MAIN, WIDE))
        got += nn(dlogits, router[:, columns])
        got *= gain[:, columns].astype(F32)
        scaled[:, columns] = got
        return dot + jnp.sum(got * saved[:, columns].astype(F32), axis=1, keepdims=True)

    with scope("finish_b"):
        dot = lax.fori_loop(0, PARTS, grad_in, jnp.zeros((T, 1), F32)) * (1.0 / D)
    back = inv * inv * inv * dot

    def finish_b(q, _):
        columns = pl.ds(pl.multiple_of(q * WIDE, 128), WIDE)
        dx = inv * scaled[:, columns] - saved[:, columns].astype(F32) * back
        saved[:, columns] = (arr_b[:, columns].astype(F32) + dx).astype(BF16)
        return 0

    with scope("finish_b2"):
        lax.fori_loop(0, PARTS, finish_b, 0)
    out_b = pltpu.make_async_copy(saved, ob_hbm, osem.at[0])
    out_b.start()
    pieces = [pl.ds(i * (D // 2), D // 2) for i in (0, 1)]
    out_f = [pltpu.make_async_copy(normed.at[:, piece], of_hbm.at[:, piece], osem.at[1 + i]) for i, piece in enumerate(pieces)]

    places_f = [colf[:, p : p + 1] for p in range(4)]
    weight_f = [gf[:, 0:1], gf[:, 1:2]]
    main_f = spread(places_f[0:2], weight_f, 0.0)
    def finish_f(q, _):
        columns = pl.ds(pl.multiple_of(q * WIDE, 128), WIDE)
        over_w = spread(places_f[2:4], weight_f, (OVER * q).astype(F32))
        got = nn(main_f, r2r[:, pl.ds(pl.multiple_of(q * MAIN + MAIN, MAIN), MAIN), :].reshape(E * MAIN, WIDE))
        got += nn(over_w, r2r[:, 0:MAIN, :].reshape(E * MAIN, WIDE))
        normed[:, columns] = (arr_f[:, columns].astype(F32) + got).astype(BF16)
        return 0

    with scope("finish_f"):
        arrive(5, a2s, r2r)
        lax.fori_loop(0, PARTS // 2, finish_f, 0)
        out_f[0].start()
        arrive(6, a2s, r2r)
        lax.fori_loop(PARTS // 2, PARTS, finish_f, 0)
        out_f[1].start()
    with scope("drain"):
        hop_sent(0)
        hop_sent(1)
        sent(2, a3s, a3r)
        sent(3, ps, pr)
        sent(4, a1s, r1r)
        sent(5, a2s, r2r)
        sent(6, a2s, r2r)
        out_b.wait()
        out_f[0].wait()
        out_f[1].wait()


def leave(f_hbm, b_hbm, of_hbm, ob_hbm, f_ref, b_ref, in_sem, out_sem):
    pairs = []
    for i, (src, mid, dst) in enumerate(((f_hbm, f_ref, of_hbm), (b_hbm, b_ref, ob_hbm))):
        for j in range(4):
            part = pl.ds(j * (T // 4), T // 4)
            pairs.append(
                (pltpu.make_async_copy(src.at[part], mid.at[part], in_sem.at[i, j]),
                 pltpu.make_async_copy(mid.at[part], dst.at[part], out_sem.at[i, j]))
            )
    for come, _ in pairs:
        come.start()
    for come, go in pairs:
        come.wait()
        go.start()
    for _, go in pairs:
        go.wait()


def per_device(fwd_acts, bwd_saved, bwd_cot, fwd_ids, bwd_ids, norm_gain, router, w_gate, w_up, w_down):
    def vm(*shape, dtype=BF16):
        return pltpu.VMEM(shape, dtype)

    block = (E, BLOCK, WIDE)
    scratch = [
        vm(D, H), vm(D, H), vm(H, D),
        *[vm(*block) for _ in range(8)],
        vm(E, MAIN, T), vm(E, MAIN, T),
        vm(ROWS, D),
        *[vm(T, D) for _ in range(4)],
        vm(ROWS, H), vm(ROWS, H), vm(ROWS, H, dtype=F32), vm(ROWS, H, dtype=F32),
        vm(T, D, dtype=F32),
        vm(E, D), vm(1, D),
        vm(2, T, dtype=jnp.int32), vm(2, T, dtype=jnp.int32),
        *[vm(8, T, dtype=F32) for _ in range(2)],
        *[vm(T, T, dtype=F32) for _ in range(4)],
        vm(2, QUARTER, D),
        pltpu.SemaphoreType.DMA((7, E)), pltpu.SemaphoreType.DMA((7, E)),
        pltpu.SemaphoreType.DMA((2, XS)), pltpu.SemaphoreType.DMA((2, XS)),
        pltpu.SemaphoreType.DMA((2,)), pltpu.SemaphoreType.DMA((2,)),
        pltpu.SemaphoreType.DMA((8,)), pltpu.SemaphoreType.DMA((3,)),
    ]
    out = jax.ShapeDtypeStruct((T, D), BF16)
    fwd_out, bwd_grad = pl.pallas_call(
        kernel,
        out_shape=(out, out),
        in_specs=[pl.BlockSpec(memory_space=pltpu.HBM)] * 10,
        out_specs=(pl.BlockSpec(memory_space=pltpu.HBM),) * 2,
        scratch_shapes=scratch,
        name="layer",
        compiler_params=pltpu.CompilerParams(
            collective_id=0, has_side_effects=True, vmem_limit_bytes=62 * 1024 * 1024
        ),
        cost_estimate=pl.CostEstimate(flops=8 * 2 * ROWS * D * H, bytes_accessed=30_000_000, transcendentals=0),
    )(
        fwd_acts[0], bwd_saved[0], bwd_cot[0], fwd_ids[0].T, bwd_ids[0].T, norm_gain, router[0].T,
        w_gate[0, 0], w_up[0, 0], w_down[0, 0],
    )
    fwd_out, bwd_grad = pl.pallas_call(
        leave,
        out_shape=(out, out),
        in_specs=[pl.BlockSpec(memory_space=pltpu.HBM)] * 2,
        out_specs=(pl.BlockSpec(memory_space=pltpu.HBM),) * 2,
        scratch_shapes=[vm(T, D), vm(T, D), pltpu.SemaphoreType.DMA((2, 4)), pltpu.SemaphoreType.DMA((2, 4))],
        name="leave",
        cost_estimate=pl.CostEstimate(flops=0, bytes_accessed=4 * 2 * T * D, transcendentals=0),
    )(fwd_out, bwd_grad)
    return fwd_out[None], bwd_grad[None]


def solution(mesh):
    rows = P("section", "expert", None)
    return jax.shard_map(
        per_device,
        mesh=mesh,
        in_specs=(
            rows, rows, rows, rows, rows, P("section", None), P("section", None, None),
            P("section", "expert", None, None), P("section", "expert", None, None), P("section", "expert", None, None),
        ),
        out_specs=(rows, rows),
        check_vma=False,
    )
```
